256 devices in a mesh: pipe: 64 (over z_lo, x, y), tp: 4 (over z_hi, core).
Axes of the slice: x: 4, y: 4, z: 8 (z_hi: 2, z_lo: 4; z = z_hi * 4 + z_lo), core: 2. Of those that a mesh axis runs over, the one named last changes fastest.
Arguments:
- hidden_stash: bfloat16 [64, 512, 8192], P('pipe', None, 'tp'), may hold values from -6 to 6
- key_stash: bfloat16 [64, 512, 512], P('pipe', None, 'tp'), may hold values from -6 to 6
- value_stash: bfloat16 [64, 512, 512], P('pipe', None, 'tp'), may hold values from -4 to 4
- top_grads: bfloat16 [512, 8192], P(None, 'tp'), may hold values from -1400 to 1400
- response_lengths: int32 [4], replicated, may hold values from 1 to 64, 192 in all
Outputs:
- kv_grads: float32 [64, 512, 1024], P('pipe', None, 'tp')
The draws below stay inside these ranges and needn't reach their ends.
Inputs may be any that keep to these rules, and one draw needn't show every extreme that they name: `response_lengths`: one response has exactly 64 live tokens; the lengths sum to 192.
All inputs are finite; a program needn't handle non-finite values.
Results may differ from the reference program's by a relative error of at most 0.012.
The reference program's roundings to bfloat16 on the way count: a program that leaves them out, or rounds other values in their place, can miss the bound.
Values may be sent and summed in bfloat16 or wider, within the bound.
No kernel may reach another device: no remote copies, remote signals or barrier semaphores. Data moves between devices by JAX's collectives and lax.ppermute only.
A program may use at most 64 MiB of HBM per device.

```python
import math
import jax
import jax.numpy as jnp
import numpy as np
from jax import lax

HEADS = 64
KVH = 4
HD = 128
PROMPT = 256
NRESP = 4
RLEN = 64
TOK = 512
LAYERS = 64


def draw_hidden_stash(key, part):
    key = jax.random.fold_in(key, 101)
    shape_full = (LAYERS, TOK, HEADS, HD)
    base = jax.random.truncated_normal(key, -6.0, 6.0, shape_full, jnp.float32)
    return base.reshape(LAYERS, TOK, HEADS * HD).astype(jnp.bfloat16)


def draw_key_stash(key, part):
    key = jax.random.fold_in(key, 202)
    shape_full = (LAYERS, TOK, KVH, HD)
    base = jax.random.truncated_normal(key, -6.0, 6.0, shape_full, jnp.float32)
    return base.reshape(LAYERS, TOK, KVH * HD).astype(jnp.bfloat16)


def draw_value_stash(key, part):
    key = jax.random.fold_in(key, 303)
    shape_full = (LAYERS, TOK, KVH * HD)
    layer_pos = jnp.arange(LAYERS, dtype=jnp.float32) / max(LAYERS - 1, 1)
    layer_scale = 0.2 * 3.0 ** (1.0 - layer_pos)
    base = jax.random.truncated_normal(key, -6.0, 6.0, shape_full, jnp.float32)
    return (base * layer_scale[:, None, None]).astype(jnp.bfloat16)


def draw_top_grads(key, part):
    key = jax.random.fold_in(key, 404)
    noise_key, row_key, column_key = jax.random.split(key, 3)
    width = HEADS * HD
    row_scale = jnp.exp(jax.random.uniform(row_key, (TOK, 1), jnp.float32, 0.0, math.log(4.0)))
    column_scale = jnp.exp(jax.random.uniform(column_key, (1, width), jnp.float32, 0.0, math.log(4.0)))
    base = jax.random.truncated_normal(noise_key, -6.0, 6.0, (TOK, width), jnp.float32)
    return (4.0 * base * row_scale * column_scale).astype(jnp.bfloat16)


def profile(number_of, total, limit, slope):
    portions = [(1 << 20) // math.isqrt(standing ** slope) + 1 for standing in range(2, number_of + 1)]
    spare, given = total - limit - (number_of - 1), [1] * (number_of - 1)
    while spare > 0:
        free = [i for i in range(number_of - 1) if given[i] < limit]
        whole, remaining = sum([portions[i] for i in free]), spare
        for i in free:
            addition = min(limit - given[i], max(1, remaining * portions[i] // whole), spare)
            given[i] = given[i] + addition
            spare = spare - addition
    return np.array([limit] + given)


def uneven(stream_key, amount, total, bound, slope):
    if amount == 2:
        one = jax.random.randint(stream_key, (), max(1, total - bound), min(bound, total - 1) + 1)
        return jnp.stack([one, total - one])
    sizes = jnp.asarray(profile(amount, total, bound, slope), jnp.int32)
    couples = (amount - 1) // 2
    donor, taker = sizes[1:1 + 2 * couples:2], sizes[2:2 + 2 * couples:2]
    margin = jnp.minimum(donor - 1, bound - taker)
    moved = jax.random.randint(jax.random.fold_in(stream_key, 1), (couples,), 0, 1 << 20) % (margin + 1)
    sizes = sizes.at[1:1 + 2 * couples:2].set(donor - moved).at[2:2 + 2 * couples:2].set(taker + moved)
    return sizes[jax.random.permutation(jax.random.fold_in(stream_key, 2), amount)]


def setup_inputs(seed: int = 0) -> dict:
    seeds = jax.random.split(jax.random.key(seed), 6)
    return {
        "hidden_stash": draw_hidden_stash(jax.random.fold_in(seeds[5], 71), 0),
        "key_stash": draw_key_stash(jax.random.fold_in(seeds[5], 71), 0),
        "value_stash": draw_value_stash(jax.random.fold_in(seeds[5], 71), 0),
        "top_grads": draw_top_grads(jax.random.fold_in(seeds[5], 71), 0),
        "response_lengths": uneven(seeds[4], NRESP, 3 * NRESP * RLEN // 4, RLEN, 1).astype(jnp.int32),
    }


clip_rms = 0.5

def live_rows(response_lengths):
    positions = jnp.arange(TOK, dtype=jnp.int32)
    response_slot = jnp.clip((positions - PROMPT) // RLEN, 0, NRESP - 1).astype(jnp.int32)
    offset_in = positions - PROMPT - response_slot * RLEN
    return (positions < PROMPT) | (offset_in < response_lengths[response_slot])

def visible_pairs(query_rows, live_flags):
    positions = jnp.arange(TOK, dtype=jnp.int32)
    query_col = query_rows[:, None]
    key_row = positions[None, :]
    causal_ok = key_row <= query_col
    in_prompt = key_row < PROMPT
    prompt_part = in_prompt & ((query_col >= PROMPT) | causal_ok)
    same_slot = (query_col - PROMPT) // RLEN == (key_row - PROMPT) // RLEN
    reply_part = ~in_prompt & (query_col >= PROMPT) & same_slot & causal_ok
    return live_flags[None, :] & (prompt_part | reply_part)

def layer_backward(query_bf, key_bf, value_bf, grad_bf, visible_mask):
    score_scale = 1.0 / math.sqrt(HD)
    queries = query_bf.astype(jnp.float32)
    key_vals = key_bf.astype(jnp.float32)
    value_vals = value_bf.astype(jnp.float32)
    grad_vals = grad_bf.astype(jnp.float32)
    scores = jnp.einsum('qgnd,kgd->gnqk', queries, key_vals) * score_scale
    scores = jnp.where(visible_mask[None, None], scores, -jnp.inf)
    row_max = lax.optimization_barrier(jnp.max(scores, axis=-1, keepdims=True))
    weights = jnp.exp(scores - row_max)
    probability = weights / lax.optimization_barrier(jnp.sum(weights, axis=-1, keepdims=True))
    probability_bf = lax.optimization_barrier(probability.astype(jnp.bfloat16)).astype(jnp.float32)
    attended = jnp.einsum('gnqk,kgd->qgnd', probability_bf, value_vals)
    row_delta = lax.optimization_barrier(jnp.sum(grad_vals * attended, axis=-1))
    dprobs = jnp.einsum('qgnd,kgd->gnqk', grad_vals, value_vals)
    dscores = probability * (dprobs - jnp.transpose(row_delta, (1, 2, 0))[..., None])
    dscores_bf = lax.optimization_barrier(dscores.astype(jnp.bfloat16)).astype(jnp.float32)
    query_grad = jnp.einsum('gnqk,kgd->qgnd', dscores_bf, key_vals) * score_scale
    key_grad = jnp.einsum('gnqk,qgnd->kgd', dscores_bf, queries) * score_scale
    value_grad = jnp.einsum('gnqk,qgnd->kgd', probability_bf, grad_vals)
    return (query_grad, key_grad, value_grad)

def reference(hidden_stash, key_stash, value_stash, top_grads, response_lengths):
    live_flags = live_rows(response_lengths)
    visible_mask = visible_pairs(jnp.arange(TOK, dtype=jnp.int32), live_flags)
    group_size = HEADS // KVH
    start_grad = jnp.where(live_flags[:, None], top_grads, jnp.zeros_like(top_grads))

    def one_layer(grad_now, layer_in):
        stash_layer, key_layer, value_layer = layer_in
        query_grad, key_grad, value_grad = layer_backward(stash_layer.reshape(TOK, KVH, group_size, HD), key_layer.reshape(TOK, KVH, HD), value_layer.reshape(TOK, KVH, HD), grad_now.reshape(TOK, KVH, group_size, HD), visible_mask)
        grad_next = (grad_now.astype(jnp.float32) + query_grad.reshape(TOK, HEADS * HD)).astype(jnp.bfloat16)
        paired = jnp.stack([key_grad, value_grad], axis=2).reshape(TOK, KVH * 2 * HD)
        return (grad_next, paired)
    last_grad, raw_grads = lax.scan(one_layer, start_grad, (hidden_stash, key_stash, value_stash), reverse=True)
    square_sum = jnp.sum(raw_grads * raw_grads)
    clip_limit = clip_rms * math.sqrt(LAYERS * TOK * 2 * KVH * HD)
    factor = clip_limit / jnp.maximum(jnp.sqrt(square_sum), clip_limit)
    return raw_grads * factor
```

```python
import math

import jax
import jax.numpy as jnp
from jax import lax
from jax.experimental import pallas as pl
from jax.experimental.pallas import tpu as pltpu
from jax.sharding import Mesh, PartitionSpec as P

HD = 128
PROMPT = 256
NRESP = 4
RLEN = 64
RESP = 192
LIVE = PROMPT + RESP
STAGES = 4
SIDE = 4
PLANE = SIDE * SIDE

clip_rms = 0.5
SCALE = 1.0 / math.sqrt(HD)
EXP2_SCALE = SCALE * math.log2(math.e)
f32 = jnp.float32
bf16 = jnp.bfloat16


def dot(a, b):
    return lax.dot_general(a, b, (((1,), (0,)), ((), ())), preferred_element_type=f32)


def dot_nt(a, b):
    return lax.dot_general(a, b, (((1,), (1,)), ((), ())), preferred_element_type=f32)


def params():
    return pltpu.CompilerParams(vmem_limit_bytes=48 << 20)


def shape(dims, dtype=f32):
    return jax.ShapeDtypeStruct(dims, dtype)


def starts(lens):
    first = lens[0]
    second = first + lens[1]
    return first, second, second + lens[2]


def start_of(row, lens):
    one, two, three = starts(lens)
    return jnp.where(
        row >= three, three, jnp.where(row >= two, two, jnp.where(row >= one, one, 0))
    )


def prompt_bias(query_dim):
    q = lax.broadcasted_iota(jnp.int32, (PROMPT, PROMPT), query_dim)
    k = lax.broadcasted_iota(jnp.int32, (PROMPT, PROMPT), 1 - query_dim)
    return jnp.where(k <= q, 0.0, -jnp.inf).astype(f32)


def response_bias(lens, query_dim):
    q = lax.broadcasted_iota(jnp.int32, (RESP, RESP), query_dim)
    k = lax.broadcasted_iota(jnp.int32, (RESP, RESP), 1 - query_dim)
    return jnp.where((k <= q) & (k >= start_of(q, lens)), 0.0, -jnp.inf).astype(f32)


def chosen_rows(lens, row_dim):
    dims = (RESP, NRESP * RLEN) if row_dim == 0 else (NRESP * RLEN, RESP)
    row = lax.broadcasted_iota(jnp.int32, dims, row_dim)
    col = lax.broadcasted_iota(jnp.int32, dims, 1 - row_dim)
    one, two, three = starts(lens)
    slot = (
        (row >= one).astype(jnp.int32)
        + (row >= two).astype(jnp.int32)
        + (row >= three).astype(jnp.int32)
    )
    return jnp.where(col == slot * RLEN + row - start_of(row, lens), 1.0, 0.0).astype(bf16)


def pack_kernel(lens, place, x_ref, top_ref, key_ref, value_ref, xp_out, xr_out, tp_out, tr_out, k_out, v_out):
    chosen = chosen_rows(lens, 0)
    for h in range(x_ref.shape[1] // HD):
        cols = slice(h * HD, (h + 1) * HD)
        xp_out[h] = x_ref[:PROMPT, cols]
        xr_out[h] = dot(chosen, x_ref[PROMPT:, cols]).astype(bf16)
    tp_out[...] = top_ref[:PROMPT]
    tr_out[...] = dot(chosen, top_ref[PROMPT:]).astype(bf16)
    for ref, out in ((key_ref, k_out), (value_ref, v_out)):
        out[:PROMPT] = ref[:PROMPT]
        out[PROMPT:] = dot(chosen, ref[PROMPT:]).astype(bf16)


def pack(lens, place, x, top, key, value):
    rows, width = x.shape
    heads = width // HD
    whole = lambda *dims: pl.BlockSpec(dims, lambda i, l, p: (0,) * len(dims))
    return pl.pallas_call(
        pack_kernel,
        name="pack",
        grid_spec=pltpu.PrefetchScalarGridSpec(
            num_scalar_prefetch=2,
            grid=(1,),
            in_specs=[
                whole(rows, width),
                pl.BlockSpec((rows, HD), lambda i, l, p: (0, p[0])),
                whole(rows, HD),
                whole(rows, HD),
            ],
            out_specs=[
                whole(heads, PROMPT, HD),
                whole(heads, RESP, HD),
                whole(PROMPT, HD),
                whole(RESP, HD),
                whole(LIVE, HD),
                whole(LIVE, HD),
            ],
        ),
        out_shape=[
            shape((heads, PROMPT, HD), bf16),
            shape((heads, RESP, HD), bf16),
            shape((PROMPT, HD), bf16),
            shape((RESP, HD), bf16),
            shape((LIVE, HD), bf16),
            shape((LIVE, HD), bf16),
        ],
        compiler_params=params(),
    )(lens, place, x, top, key, value)


def prompt_prob_kernel(lens, ks, vs, q_ref, k_ref, v_ref, prob_ref, att_ref, bias):
    @pl.when(pl.program_id(0) == 0)
    def _():
        bias[...] = prompt_bias(0)

    s = dot_nt(q_ref[0], k_ref[0]) + bias[...]
    m = jnp.max(s, -1, keepdims=True)
    w = jnp.exp2((s - m) * EXP2_SCALE)
    p = w * (1.0 / jnp.sum(w, -1, keepdims=True))
    prob_ref[0] = p
    att_ref[0] = dot(p.astype(bf16), v_ref[0])


def prompt_prob(lens, ks, vs, q, k, v):
    n = q.shape[0]
    block = lambda *dims: pl.BlockSpec((1,) + dims, lambda l, a, b, c: (l, 0, 0))
    return pl.pallas_call(
        prompt_prob_kernel,
        name="prompt_prob",
        grid_spec=pltpu.PrefetchScalarGridSpec(
            num_scalar_prefetch=3,
            grid=(n,),
            in_specs=[
                block(PROMPT, HD),
                pl.BlockSpec((1, PROMPT, HD), lambda l, a, b, c: (b[l], 0, 0)),
                pl.BlockSpec((1, PROMPT, HD), lambda l, a, b, c: (c[l], 0, 0)),
            ],
            out_specs=[block(PROMPT, PROMPT), block(PROMPT, HD)],
            scratch_shapes=[pltpu.VMEM((PROMPT, PROMPT), f32)],
        ),
        out_shape=[shape((n, PROMPT, PROMPT)), shape((n, PROMPT, HD))],
        compiler_params=params(),
    )(lens, ks, vs, q, k, v)


def response_prob_kernel(lens, ks, vs, q_ref, k_ref, v_ref, first_ref, own_ref, att_ref, bias):
    @pl.when(pl.program_id(0) == 0)
    def _():
        bias[...] = response_bias(lens, 0)

    q = q_ref[0]
    k = k_ref[0]
    v = v_ref[0]
    s1 = dot_nt(q, k[:PROMPT])
    s2 = dot_nt(q, k[PROMPT:]) + bias[...]
    m = jnp.maximum(jnp.max(s1, -1, keepdims=True), jnp.max(s2, -1, keepdims=True))
    w1 = jnp.exp2((s1 - m) * EXP2_SCALE)
    w2 = jnp.exp2((s2 - m) * EXP2_SCALE)
    r = 1.0 / (jnp.sum(w1, -1, keepdims=True) + jnp.sum(w2, -1, keepdims=True))
    p1 = w1 * r
    p2 = w2 * r
    first_ref[0] = p1
    own_ref[0] = p2
    att_ref[0] = dot(p1.astype(bf16), v[:PROMPT]) + dot(p2.astype(bf16), v[PROMPT:])


def response_prob(lens, ks, vs, q, k, v):
    n = q.shape[0]
    block = lambda *dims: pl.BlockSpec((1,) + dims, lambda l, a, b, c: (l, 0, 0))
    return pl.pallas_call(
        response_prob_kernel,
        name="response_prob",
        grid_spec=pltpu.PrefetchScalarGridSpec(
            num_scalar_prefetch=3,
            grid=(n,),
            in_specs=[
                block(RESP, HD),
                pl.BlockSpec((1, LIVE, HD), lambda l, a, b, c: (b[l], 0, 0)),
                pl.BlockSpec((1, LIVE, HD), lambda l, a, b, c: (c[l], 0, 0)),
            ],
            out_specs=[block(RESP, PROMPT), block(RESP, RESP), block(RESP, HD)],
            scratch_shapes=[pltpu.VMEM((RESP, RESP), f32)],
        ),
        out_shape=[shape((n, RESP, PROMPT)), shape((n, RESP, RESP)), shape((n, RESP, HD))],
        compiler_params=params(),
    )(lens, ks, vs, q, k, v)


def prompt_chain_kernel(ks, vs, g_ref, prob_ref, att_ref, k_ref, v_ref, stash_ref, out_ref):
    @pl.when(pl.program_id(0) == 0)
    def _():
        out_ref[...] = g_ref[...]

    d = out_ref[...]
    stash_ref[0] = d
    wide = d.astype(f32)
    delta = jnp.sum(wide * att_ref[0], -1, keepdims=True)
    ds = (prob_ref[0] * (dot_nt(d, v_ref[0]) - delta)).astype(bf16)
    out_ref[...] = (wide + dot(ds, k_ref[0]) * SCALE).astype(bf16)


def response_chain_kernel(ks, vs, g_ref, first_ref, own_ref, att_ref, k_ref, v_ref, stash_ref, out_ref):
    @pl.when(pl.program_id(0) == 0)
    def _():
        out_ref[...] = g_ref[...]

    d = out_ref[...]
    stash_ref[0] = d
    wide = d.astype(f32)
    k = k_ref[0]
    v = v_ref[0]
    delta = jnp.sum(wide * att_ref[0], -1, keepdims=True)
    ds1 = (first_ref[0] * (dot_nt(d, v[:PROMPT]) - delta)).astype(bf16)
    ds2 = (own_ref[0] * (dot_nt(d, v[PROMPT:]) - delta)).astype(bf16)
    step = dot(ds1, k[:PROMPT]) + dot(ds2, k[PROMPT:])
    out_ref[...] = (wide + step * SCALE).astype(bf16)


def chain(kernel, name, ks, vs, g, probs, k, v):
    n = probs[0].shape[0]
    rows = g.shape[0]
    keys = probs[0].shape[2] if len(probs) == 2 else LIVE
    block = lambda *dims: pl.BlockSpec((1,) + dims, lambda i, a, b: (n - 1 - i, 0, 0))
    whole = pl.BlockSpec((rows, HD), lambda i, a, b: (0, 0))
    return pl.pallas_call(
        kernel,
        name=name,
        grid_spec=pltpu.PrefetchScalarGridSpec(
            num_scalar_prefetch=2,
            grid=(n,),
            in_specs=[whole]
            + [block(*p.shape[1:]) for p in probs]
            + [
                pl.BlockSpec((1, keys, HD), lambda i, a, b: (a[n - 1 - i], 0, 0)),
                pl.BlockSpec((1, keys, HD), lambda i, a, b: (b[n - 1 - i], 0, 0)),
            ],
            out_specs=[block(rows, HD), whole],
        ),
        out_shape=[shape((n, rows, HD), bf16), shape((rows, HD), bf16)],
        compiler_params=params(),
    )(ks, vs, g, *probs, k, v)


def kv_grad_kernel(lens, qp_ref, qr_ref, gp_ref, gr_ref, k_ref, v_ref, out_ref, sum_ref, bias_p, bias_r, acc):
    h = pl.program_id(0)

    @pl.when(h == 0)
    def _():
        bias_p[...] = prompt_bias(1)
        bias_r[...] = response_bias(lens, 1)
        acc[...] = jnp.zeros_like(acc)

    qp, qr, gp, gr = qp_ref[0], qr_ref[0], gp_ref[0], gr_ref[0]
    k1, k2 = k_ref[:PROMPT], k_ref[PROMPT:]
    v1, v2 = v_ref[:PROMPT], v_ref[PROMPT:]
    s = dot_nt(k1, qp) + bias_p[...]
    dp = dot_nt(v1, gp)
    w = jnp.exp2((s - jnp.max(s, 0, keepdims=True)) * EXP2_SCALE)
    p = w * (1.0 / jnp.sum(w, 0, keepdims=True))
    pb = p.astype(bf16)
    delta = jnp.sum(pb.astype(f32) * dp, 0, keepdims=True)
    ds = (p * (dp - delta)).astype(bf16)
    s1 = dot_nt(k1, qr)
    s2 = dot_nt(k2, qr) + bias_r[...]
    dp1 = dot_nt(v1, gr)
    dp2 = dot_nt(v2, gr)
    m = jnp.maximum(jnp.max(s1, 0, keepdims=True), jnp.max(s2, 0, keepdims=True))
    w1 = jnp.exp2((s1 - m) * EXP2_SCALE)
    w2 = jnp.exp2((s2 - m) * EXP2_SCALE)
    r = 1.0 / (jnp.sum(w1, 0, keepdims=True) + jnp.sum(w2, 0, keepdims=True))
    p1 = w1 * r
    p2 = w2 * r
    pb1 = p1.astype(bf16)
    pb2 = p2.astype(bf16)
    delta = jnp.sum(pb1.astype(f32) * dp1, 0, keepdims=True) + jnp.sum(
        pb2.astype(f32) * dp2, 0, keepdims=True
    )
    ds1 = (p1 * (dp1 - delta)).astype(bf16)
    ds2 = (p2 * (dp2 - delta)).astype(bf16)
    acc[:PROMPT, :HD] += (dot(ds, qp) + dot(ds1, qr)) * SCALE
    acc[PROMPT:, :HD] += dot(ds2, qr) * SCALE
    acc[:PROMPT, HD:] += dot(pb, gp) + dot(pb1, gr)
    acc[PROMPT:, HD:] += dot(pb2, gr)

    @pl.when(h == pl.num_programs(0) - 1)
    def _():
        total = acc[...]
        squares = jnp.sum(total * total, 0, keepdims=True)
        sum_ref[...] = squares[:, :HD] + squares[:, HD:]
        out_ref[:PROMPT] = total[:PROMPT]
        spread = chosen_rows(lens, 1)
        left = total[PROMPT:]
        placed = jnp.zeros((NRESP * RLEN, 2 * HD), f32)
        for _ in range(3):
            term = left.astype(bf16)
            placed = placed + dot(spread, term)
            left = left - term.astype(f32)
        out_ref[PROMPT:] = placed


def kv_grad(lens, qp, qr, gp, gr, k, v):
    n = qp.shape[0]
    rows = PROMPT + NRESP * RLEN
    block = lambda *dims: pl.BlockSpec((1,) + dims, lambda i, a: (i, 0, 0))
    whole = lambda *dims: pl.BlockSpec(dims, lambda i, a: (0, 0))
    return pl.pallas_call(
        kv_grad_kernel,
        name="kv_grad",
        grid_spec=pltpu.PrefetchScalarGridSpec(
            num_scalar_prefetch=1,
            grid=(n,),
            in_specs=[
                block(PROMPT, HD),
                block(RESP, HD),
                block(PROMPT, HD),
                block(RESP, HD),
                whole(LIVE, HD),
                whole(LIVE, HD),
            ],
            out_specs=[whole(rows, 2 * HD), whole(1, HD)],
            scratch_shapes=[
                pltpu.VMEM((PROMPT, PROMPT), f32),
                pltpu.VMEM((RESP, RESP), f32),
                pltpu.VMEM((LIVE, 2 * HD), f32),
            ],
        ),
        out_shape=[shape((rows, 2 * HD)), shape((1, HD))],
        compiler_params=params(),
    )(lens, qp, qr, gp, gr, k, v)


def ring(step, size=SIDE):
    return [(i, (i + step) % size) for i in range(size)]


def gathered(block, axis):
    low = lax.ppermute(block, axis, ring(1))
    high = lax.ppermute(block, axis, ring(-1))
    half = block.shape[0] // 2
    far = jnp.concatenate(
        [
            lax.ppermute(low[:half], axis, ring(1)),
            lax.ppermute(high[half:], axis, ring(-1)),
        ]
    )
    return jnp.stack([block, low, high, far])


def slot_of(distance):
    distance = distance % SIDE
    return jnp.where(distance == 0, 0, jnp.where(distance == SIDE - 1, 1, distance + 1))


def on_device(hidden_stash, key_stash, value_stash, top_grads, lens):
    stage = lax.axis_index("zl")
    my_x = lax.axis_index("x")
    my_y = lax.axis_index("y")
    place = (my_x * SIDE + my_y).reshape(1).astype(jnp.int32)
    qp, qr, tp, tr, k, v = pack(
        lens, place, hidden_stash[0], top_grads, key_stash[0], value_stash[0]
    )
    layers = jnp.arange(PLANE, dtype=jnp.int32)
    slot_x = slot_of(layers // SIDE - my_x)
    slot_y = slot_of(layers % SIDE - my_y)
    ks = (slot_x * SIDE + slot_y).astype(jnp.int32)
    vs = (slot_y * SIDE + slot_x).astype(jnp.int32)
    all_k = gathered(gathered(k, "y"), "x").reshape(PLANE, LIVE, HD)
    all_v = gathered(gathered(v, "x"), "y").reshape(PLANE, LIVE, HD)
    plane = ("x", "y")
    my_qp = lax.all_to_all(qp, plane, 0, 0, tiled=True)
    my_qr = lax.all_to_all(qr, plane, 0, 0, tiled=True)
    prob_p = prompt_prob(lens, ks, vs, my_qp, all_k, all_v)
    prob_r = response_prob(lens, ks, vs, my_qr, all_k, all_v)
    gp, gr = tp, tr
    stash_p = jnp.zeros((PLANE, PROMPT, HD), bf16)
    stash_r = jnp.zeros((PLANE, RESP, HD), bf16)
    for now in range(STAGES - 1, -1, -1):
        mine = stage == now

        def run_p(g, stash):
            return tuple(chain(prompt_chain_kernel, "prompt_chain", ks, vs, g, prob_p, all_k, all_v))

        def run_r(g, stash):
            return tuple(chain(response_chain_kernel, "response_chain", ks, vs, g, prob_r, all_k, all_v))

        def idle(g, stash):
            return (stash, g)

        stash_p, gp = lax.cond(mine, run_p, idle, gp, stash_p)
        stash_r, gr = lax.cond(mine, run_r, idle, gr, stash_r)
        if now:
            gp = lax.ppermute(gp, "zl", [(now, now - 1)])
            gr = lax.ppermute(gr, "zl", [(now, now - 1)])
    own_gp = lax.all_to_all(stash_p, plane, 0, 0, tiled=True)
    own_gr = lax.all_to_all(stash_r, plane, 0, 0, tiled=True)
    raw, squares = kv_grad(lens, qp, qr, own_gp, own_gr, k, v)
    for axes, size in ((plane, PLANE), (("zl", "tp"), STAGES * lax.axis_size("tp"))):
        spread = jnp.broadcast_to(squares, (size, HD))
        squares = jnp.sum(lax.all_to_all(spread, axes, 0, 0, tiled=True), 0, keepdims=True)
    square_sum = jnp.sum(squares)
    entries = STAGES * PLANE * lax.axis_size("tp") * raw.shape[0] * raw.shape[1]
    clip_limit = clip_rms * math.sqrt(entries)
    factor = clip_limit / jnp.maximum(jnp.sqrt(square_sum), clip_limit)
    return (raw * factor)[None]


def solution(mesh):
    parts = mesh.devices.reshape(STAGES, SIDE, SIDE, -1)
    finer = Mesh(parts, ("zl", "x", "y", "tp"))
    pipe = ("zl", "x", "y")
    placed = (
        P(pipe, None, "tp"),
        P(pipe, None, "tp"),
        P(pipe, None, "tp"),
        P(None, "tp"),
        P(),
    )
    return jax.shard_map(
        on_device, mesh=finer, in_specs=placed, out_specs=P(pipe, None, "tp"), check_vma=False
    )
```

```python
import functools
import math

import jax
import jax.numpy as jnp
from jax import lax
from jax.experimental import pallas as pl
from jax.experimental.pallas import tpu as pltpu
from jax.sharding import Mesh, PartitionSpec as P

HD = 128
PROMPT = 256
NRESP = 4
RLEN = 64
RESP = 192
LIVE = PROMPT + RESP
STAGES = 4
SIDE = 4
PLANE = SIDE * SIDE

clip_rms = 0.5
SCALE = 1.0 / math.sqrt(HD)
EXP2_SCALE = SCALE * math.log2(math.e)
f32 = jnp.float32
bf16 = jnp.bfloat16


def dot(a, b):
    return lax.dot_general(a, b, (((1,), (0,)), ((), ())), preferred_element_type=f32)


def dot_nt(a, b):
    return lax.dot_general(a, b, (((1,), (1,)), ((), ())), preferred_element_type=f32)


def params():
    return pltpu.CompilerParams(vmem_limit_bytes=60 << 20)


def shape(dims, dtype=f32):
    return jax.ShapeDtypeStruct(dims, dtype)


def starts(lens):
    first = lens[0]
    second = first + lens[1]
    return first, second, second + lens[2]


def start_of(row, lens):
    one, two, three = starts(lens)
    return jnp.where(
        row >= three, three, jnp.where(row >= two, two, jnp.where(row >= one, one, 0))
    )


def prompt_bias(query_dim):
    q = lax.broadcasted_iota(jnp.int32, (PROMPT, PROMPT), query_dim)
    k = lax.broadcasted_iota(jnp.int32, (PROMPT, PROMPT), 1 - query_dim)
    return jnp.where(k <= q, 0.0, -jnp.inf).astype(f32)


def response_bias(lens, query_dim):
    q = lax.broadcasted_iota(jnp.int32, (RESP, RESP), query_dim)
    k = lax.broadcasted_iota(jnp.int32, (RESP, RESP), 1 - query_dim)
    return jnp.where((k <= q) & (k >= start_of(q, lens)), 0.0, -jnp.inf).astype(f32)


def chosen_rows(lens, row_dim):
    dims = (RESP, NRESP * RLEN) if row_dim == 0 else (NRESP * RLEN, RESP)
    row = lax.broadcasted_iota(jnp.int32, dims, row_dim)
    col = lax.broadcasted_iota(jnp.int32, dims, 1 - row_dim)
    one, two, three = starts(lens)
    slot = (
        (row >= one).astype(jnp.int32)
        + (row >= two).astype(jnp.int32)
        + (row >= three).astype(jnp.int32)
    )
    return jnp.where(col == slot * RLEN + row - start_of(row, lens), 1.0, 0.0).astype(bf16)


def pack_kernel(lens, place, x_ref, top_ref, key_ref, value_ref, xp_out, xr_out, tp_out, tr_out, k_out, v_out):
    chosen = chosen_rows(lens, 0)
    for h in range(x_ref.shape[1] // HD):
        cols = slice(h * HD, (h + 1) * HD)
        xp_out[h] = x_ref[:PROMPT, cols]
        xr_out[h] = dot(chosen, x_ref[PROMPT:, cols]).astype(bf16)

    @pl.when(pl.program_id(0) == 0)
    def _():
        tp_out[...] = top_ref[:PROMPT]
        tr_out[...] = dot(chosen, top_ref[PROMPT:]).astype(bf16)
        for ref, out in ((key_ref, k_out), (value_ref, v_out)):
            out[:PROMPT] = ref[:PROMPT]
            out[PROMPT:] = dot(chosen, ref[PROMPT:]).astype(bf16)


def pack(lens, place, x, top, key, value):
    rows, width = x.shape
    heads = width // HD
    steps = 4
    some = heads // steps
    whole = lambda *dims: pl.BlockSpec(dims, lambda i, l, p: (0,) * len(dims))
    return pl.pallas_call(
        pack_kernel,
        name="pack",
        grid_spec=pltpu.PrefetchScalarGridSpec(
            num_scalar_prefetch=2,
            grid=(steps,),
            in_specs=[
                pl.BlockSpec((rows, some * HD), lambda i, l, p: (0, i)),
                pl.BlockSpec((rows, HD), lambda i, l, p: (0, p[0])),
                whole(rows, HD),
                whole(rows, HD),
            ],
            out_specs=[
                pl.BlockSpec((some, PROMPT, HD), lambda i, l, p: (i, 0, 0)),
                pl.BlockSpec((some, RESP, HD), lambda i, l, p: (i, 0, 0)),
                whole(PROMPT, HD),
                whole(RESP, HD),
                whole(LIVE, HD),
                whole(LIVE, HD),
            ],
        ),
        out_shape=[
            shape((heads, PROMPT, HD), bf16),
            shape((heads, RESP, HD), bf16),
            shape((PROMPT, HD), bf16),
            shape((RESP, HD), bf16),
            shape((LIVE, HD), bf16),
            shape((LIVE, HD), bf16),
        ],
        compiler_params=params(),
    )(lens, place, x, top, key, value)


def softmax(scores, dim):
    top = functools.reduce(jnp.maximum, [jnp.max(x, dim, keepdims=True) for x in scores])
    weights = [jnp.exp2((x - top) * EXP2_SCALE) for x in scores]
    total = functools.reduce(jnp.add, [jnp.sum(w, dim, keepdims=True) for w in weights])
    share = 1.0 / total
    return [w * share for w in weights]


AT_ONCE = 4
PROMPT_ROW = PROMPT + HD
RESP_ROW = 2 * PROMPT + HD


def prob_kernel(prompt, lens, ks, vs, q_ref, *refs):
    k_refs, v_refs = refs[:AT_ONCE], refs[AT_ONCE : 2 * AT_ONCE]
    out, bias = refs[2 * AT_ONCE :]

    @pl.when(pl.program_id(0) == 0)
    def _():
        bias[...] = prompt_bias(0) if prompt else response_bias(lens, 0)

    for u in range(AT_ONCE):
        q, k, v = q_ref[u], k_refs[u][0], v_refs[u][0]
        if prompt:
            (p,) = softmax([dot_nt(q, k) + bias[...]], -1)
            out[u, :, :PROMPT] = p
            out[u, :, PROMPT:] = dot(p.astype(bf16), v)
        else:
            p1, p2 = softmax([dot_nt(q, k[:PROMPT]), dot_nt(q, k[PROMPT:]) + bias[...]], -1)
            out[u, :, :PROMPT] = p1
            out[u, :, PROMPT:LIVE] = p2
            out[u, :, 2 * PROMPT :] = dot(p1.astype(bf16), v[:PROMPT]) + dot(
                p2.astype(bf16), v[PROMPT:]
            )


def prob(prompt, lens, ks, vs, q, k, v):
    n, rows, _ = q.shape
    keys, width = (PROMPT, PROMPT_ROW) if prompt else (LIVE, RESP_ROW)
    slot = lambda which, u: pl.BlockSpec(
        (1, keys, HD), lambda i, *tables: (tables[which][i * AT_ONCE + u], 0, 0)
    )
    block = lambda w: pl.BlockSpec((AT_ONCE, rows, w), lambda i, *tables: (i, 0, 0))
    return pl.pallas_call(
        functools.partial(prob_kernel, prompt),
        name="prompt_prob" if prompt else "response_prob",
        grid_spec=pltpu.PrefetchScalarGridSpec(
            num_scalar_prefetch=3,
            grid=(n // AT_ONCE,),
            in_specs=[block(HD)]
            + [slot(1, u) for u in range(AT_ONCE)]
            + [slot(2, u) for u in range(AT_ONCE)],
            out_specs=block(width),
            scratch_shapes=[pltpu.VMEM((rows, rows), f32)],
        ),
        out_shape=shape((n, rows, width)),
        compiler_params=params(),
    )(lens, ks, vs, q, *([k] * AT_ONCE), *([v] * AT_ONCE))


AHEAD = 3


def chain_kernel(prompt, n, active, ks, vs, g_in, stash_in, prob_hbm, k_hbm, v_hbm, g_out, stash, probs, keys, values, grads, last, sems, out_sems, g_sem):
    count = keys.shape[1]

    def loads(i):
        layer = n - 1 - i
        return (
            pltpu.make_async_copy(prob_hbm.at[layer], probs.at[layer], sems.at[layer, 0]),
            pltpu.make_async_copy(k_hbm.at[ks[layer], :count], keys.at[layer], sems.at[layer, 1]),
            pltpu.make_async_copy(v_hbm.at[vs[layer], :count], values.at[layer], sems.at[layer, 2]),
        )

    def save(layer):
        return pltpu.make_async_copy(grads.at[layer], stash.at[layer], out_sems.at[layer])

    def step(i, final):
        layer = n - 1 - i
        if not final:

            @pl.when(i + AHEAD < n)
            def _():
                for copy in loads(i + AHEAD):
                    copy.start()

        for copy in loads(i):
            copy.wait()
        save(layer).start()
        d = grads[layer]
        wide = d.astype(f32)
        k, v = keys[layer], values[layer]
        if prompt:
            delta = jnp.sum(wide * probs[layer, :, PROMPT:], -1, keepdims=True)
            ds = (probs[layer, :, :PROMPT] * (dot_nt(d, v) - delta)).astype(bf16)
            change = dot(ds, k)
        else:
            delta = jnp.sum(wide * probs[layer, :, 2 * PROMPT :], -1, keepdims=True)
            ds1 = (probs[layer, :, :PROMPT] * (dot_nt(d, v[:PROMPT]) - delta)).astype(bf16)
            ds2 = (probs[layer, :, PROMPT:LIVE] * (dot_nt(d, v[PROMPT:]) - delta)).astype(bf16)
            change = dot(ds1, k[:PROMPT]) + dot(ds2, k[PROMPT:])
        g = (wide + change * SCALE).astype(bf16)
        if final:
            last[...] = g
        else:
            grads[layer - 1] = g

    @pl.when(active[0] == 1)
    def _():
        first = pltpu.make_async_copy(g_in, grads.at[n - 1], g_sem)
        first.start()
        for i in range(AHEAD):
            for copy in loads(i):
                copy.start()
        first.wait()

        def body(i, carry):
            step(i, False)
            return carry

        lax.fori_loop(0, n - 1, body, 0)
        step(n - 1, True)
        done = pltpu.make_async_copy(last, g_out, g_sem)
        done.start()

        def finish(layer, carry):
            save(layer).wait()
            return carry

        lax.fori_loop(0, n, finish, 0)
        done.wait()


def chain(prompt, active, ks, vs, g, stash, probs, k, v):
    n, rows, width = probs.shape
    count = PROMPT if prompt else LIVE
    table = pl.BlockSpec(memory_space=pltpu.SMEM)
    hbm = pl.BlockSpec(memory_space=pl.ANY)
    return pl.pallas_call(
        functools.partial(chain_kernel, prompt, n),
        name="prompt_chain" if prompt else "response_chain",
        in_specs=[table] * 3 + [hbm] * 5,
        out_specs=[hbm] * 2,
        scratch_shapes=[
            pltpu.VMEM((n, rows, width), f32),
            pltpu.VMEM((n, count, HD), bf16),
            pltpu.VMEM((n, count, HD), bf16),
            pltpu.VMEM((n, rows, HD), bf16),
            pltpu.VMEM((rows, HD), bf16),
            pltpu.SemaphoreType.DMA((n, 3)),
            pltpu.SemaphoreType.DMA((n,)),
            pltpu.SemaphoreType.DMA,
        ],
        out_shape=[shape((rows, HD), bf16), shape((n, rows, HD), bf16)],
        input_output_aliases={3: 0, 4: 1},
        compiler_params=params(),
    )(active, ks, vs, g, stash, probs, k, v)


HEADS_AT_ONCE = 2


def prompt_grad_kernel(q_ref, g_ref, k_ref, v_ref, out_ref, bias):
    @pl.when(pl.program_id(0) == 0)
    def _():
        bias[...] = prompt_bias(1)
        out_ref[...] = jnp.zeros_like(out_ref)

    k, v = k_ref[...], v_ref[...]
    dk, dv = 0.0, 0.0
    for u in range(HEADS_AT_ONCE):
        q, g = q_ref[u], g_ref[u]
        (p,) = softmax([dot_nt(k, q) + bias[...]], 0)
        dp = dot_nt(v, g)
        pb = p.astype(bf16)
        delta = jnp.sum(pb.astype(f32) * dp, 0, keepdims=True)
        ds = (p * (dp - delta)).astype(bf16)
        dk = dk + dot(ds, q)
        dv = dv + dot(pb, g)
    out_ref[:, :HD] += dk * SCALE
    out_ref[:, HD:] += dv


def prompt_grad(q, g, k, v):
    n = q.shape[0]
    block = pl.BlockSpec((HEADS_AT_ONCE, PROMPT, HD), lambda i: (i, 0, 0))
    whole = lambda w: pl.BlockSpec((PROMPT, w), lambda i: (0, 0))
    return pl.pallas_call(
        prompt_grad_kernel,
        name="prompt_grad",
        grid=(n // HEADS_AT_ONCE,),
        in_specs=[block, block, whole(HD), whole(HD)],
        out_specs=whole(2 * HD),
        scratch_shapes=[pltpu.VMEM((PROMPT, PROMPT), f32)],
        out_shape=shape((PROMPT, 2 * HD)),
        compiler_params=params(),
    )(q, g, k, v)


def response_grad_kernel(lens, q_ref, g_ref, k_ref, v_ref, part_ref, out_ref, sum_ref, bias, acc):
    i = pl.program_id(0)

    @pl.when(i == 0)
    def _():
        bias[...] = response_bias(lens, 1)
        acc[:PROMPT] = part_ref[...]
        acc[PROMPT:] = jnp.zeros((RESP, 2 * HD), f32)

    k1, k2 = k_ref[:PROMPT], k_ref[PROMPT:]
    v1, v2 = v_ref[:PROMPT], v_ref[PROMPT:]
    dk1, dk2, dv1, dv2 = 0.0, 0.0, 0.0, 0.0
    for u in range(HEADS_AT_ONCE):
        q, g = q_ref[u], g_ref[u]
        p1, p2 = softmax([dot_nt(k1, q), dot_nt(k2, q) + bias[...]], 0)
        dp1, dp2 = dot_nt(v1, g), dot_nt(v2, g)
        pb1, pb2 = p1.astype(bf16), p2.astype(bf16)
        delta = jnp.sum(pb1.astype(f32) * dp1, 0, keepdims=True) + jnp.sum(
            pb2.astype(f32) * dp2, 0, keepdims=True
        )
        ds1 = (p1 * (dp1 - delta)).astype(bf16)
        ds2 = (p2 * (dp2 - delta)).astype(bf16)
        dk1, dk2 = dk1 + dot(ds1, q), dk2 + dot(ds2, q)
        dv1, dv2 = dv1 + dot(pb1, g), dv2 + dot(pb2, g)
    acc[:PROMPT, :HD] += dk1 * SCALE
    acc[PROMPT:, :HD] += dk2 * SCALE
    acc[:PROMPT, HD:] += dv1
    acc[PROMPT:, HD:] += dv2

    @pl.when(i == pl.num_programs(0) - 1)
    def _():
        total = acc[...]
        squares = jnp.sum(total * total, 0, keepdims=True)
        sum_ref[...] = squares[:, :HD] + squares[:, HD:]
        out_ref[:PROMPT] = total[:PROMPT]
        spread = chosen_rows(lens, 1)
        left = total[PROMPT:]
        placed = jnp.zeros((NRESP * RLEN, 2 * HD), f32)
        for _ in range(3):
            term = left.astype(bf16)
            placed = placed + dot(spread, term)
            left = left - term.astype(f32)
        out_ref[PROMPT:] = placed


def response_grad(lens, q, g, k, v, part):
    n = q.shape[0]
    rows = PROMPT + NRESP * RLEN
    block = pl.BlockSpec((HEADS_AT_ONCE, RESP, HD), lambda i, a: (i, 0, 0))
    whole = lambda *dims: pl.BlockSpec(dims, lambda i, a: (0, 0))
    return pl.pallas_call(
        response_grad_kernel,
        name="response_grad",
        grid_spec=pltpu.PrefetchScalarGridSpec(
            num_scalar_prefetch=1,
            grid=(n // HEADS_AT_ONCE,),
            in_specs=[
                block,
                block,
                whole(LIVE, HD),
                whole(LIVE, HD),
                whole(PROMPT, 2 * HD),
            ],
            out_specs=[whole(rows, 2 * HD), whole(1, HD)],
            scratch_shapes=[pltpu.VMEM((RESP, RESP), f32), pltpu.VMEM((LIVE, 2 * HD), f32)],
        ),
        out_shape=[shape((rows, 2 * HD)), shape((1, HD))],
        compiler_params=params(),
    )(lens, q, g, k, v, part)


def ring(step, size=SIDE):
    return [(i, (i + step) % size) for i in range(size)]


def gathered(block, axis):
    low = lax.ppermute(block, axis, ring(1))
    high = lax.ppermute(block, axis, ring(-1))
    half = block.shape[0] // 2
    far = jnp.concatenate(
        [
            lax.ppermute(low[:half], axis, ring(1)),
            lax.ppermute(high[half:], axis, ring(-1)),
        ]
    )
    return jnp.stack([block, low, high, far])


def slot_of(distance):
    distance = distance % SIDE
    return jnp.where(distance == 0, 0, jnp.where(distance == SIDE - 1, 1, distance + 1))


def summed(x, axis):
    size = lax.axis_size(axis)
    parts = [lax.ppermute(x, axis, ring(step, size)) for step in range(1, size)]
    return functools.reduce(jnp.add, parts, x)


def on_device(hidden_stash, key_stash, value_stash, top_grads, lens):
    stage = lax.axis_index("zl")
    my_x = lax.axis_index("x")
    my_y = lax.axis_index("y")
    place = (my_x * SIDE + my_y).reshape(1).astype(jnp.int32)
    qp, qr, gp, gr, k, v = pack(
        lens, place, hidden_stash[0], top_grads, key_stash[0], value_stash[0]
    )
    layers = jnp.arange(PLANE, dtype=jnp.int32)
    slot_x = slot_of(layers // SIDE - my_x)
    slot_y = slot_of(layers % SIDE - my_y)
    ks = (slot_x * SIDE + slot_y).astype(jnp.int32)
    vs = (slot_y * SIDE + slot_x).astype(jnp.int32)
    plane = ("x", "y")
    swap = lambda a: lax.all_to_all(a, plane, 0, 0, tiled=True)
    all_k = gathered(gathered(k, "y"), "x").reshape(PLANE, LIVE, HD)
    all_v = gathered(gathered(v, "x"), "y").reshape(PLANE, LIVE, HD)
    my_qp = swap(qp)
    my_qr = swap(lax.optimization_barrier((qr, my_qp))[0])
    prob_p = prob(True, lens, ks, vs, my_qp, all_k, all_v)
    stash_p, stash_r = my_qp, my_qr
    prob_r = None
    for now in range(STAGES - 1, -1, -1):
        active = (stage == now).astype(jnp.int32).reshape(1)
        gp, stash_p = chain(True, active, ks, vs, gp, stash_p, prob_p, all_k, all_v)
        if prob_r is None:
            my_qr, gp = lax.optimization_barrier((my_qr, gp))
            prob_r = prob(False, lens, ks, vs, my_qr, all_k, all_v)
            stash_r = my_qr
        if now:
            gp = lax.ppermute(gp, "zl", [(now, now - 1)])
        gr, stash_r = chain(False, active, ks, vs, gr, stash_r, prob_r, all_k, all_v)
        gp, gr = lax.optimization_barrier((gp, gr))
        if now:
            gr = lax.ppermute(gr, "zl", [(now, now - 1)])
    part = prompt_grad(qp, swap(stash_p), k, v)
    raw, squares = response_grad(lens, qr, swap(stash_r), k, v, part)
    for axis in ("y", "x", "tp", "zl"):
        squares = summed(squares, axis)
    square_sum = jnp.sum(squares)
    entries = STAGES * PLANE * lax.axis_size("tp") * raw.shape[0] * raw.shape[1]
    clip_limit = clip_rms * math.sqrt(entries)
    factor = clip_limit / jnp.maximum(jnp.sqrt(square_sum), clip_limit)
    return (raw * factor)[None]


def solution(mesh):
    parts = mesh.devices.reshape(STAGES, SIDE, SIDE, -1)
    finer = Mesh(parts, ("zl", "x", "y", "tp"))
    pipe = ("zl", "x", "y")
    placed = (
        P(pipe, None, "tp"),
        P(pipe, None, "tp"),
        P(pipe, None, "tp"),
        P(None, "tp"),
        P(),
    )
    return jax.shard_map(
        on_device, mesh=finer, in_specs=placed, out_specs=P(pipe, None, "tp"), check_vma=False
    )
```

```python
import functools
import math

import jax
import jax.numpy as jnp
from jax import lax
from jax.experimental import pallas as pl
from jax.experimental.pallas import tpu as pltpu
from jax.sharding import Mesh, PartitionSpec as P

HD = 128
PROMPT = 256
NRESP = 4
RLEN = 64
RESP = 192
LIVE = PROMPT + RESP
STAGES = 4
SIDE = 4
PLANE = SIDE * SIDE

clip_rms = 0.5
SCALE = 1.0 / math.sqrt(HD)
EXP2_SCALE = SCALE * math.log2(math.e)
f32 = jnp.float32
bf16 = jnp.bfloat16


def dot(a, b):
    return lax.dot_general(a, b, (((1,), (0,)), ((), ())), preferred_element_type=f32)


def dot_nt(a, b):
    return lax.dot_general(a, b, (((1,), (1,)), ((), ())), preferred_element_type=f32)


def about(us):
    return pl.CostEstimate(flops=us * 1_000_000_000, bytes_accessed=0, transcendentals=0)


def params(mebibytes=24):
    return pltpu.CompilerParams(vmem_limit_bytes=mebibytes << 20)


def shape(dims, dtype=f32):
    return jax.ShapeDtypeStruct(dims, dtype)


def starts(lens):
    first = lens[0]
    second = first + lens[1]
    return first, second, second + lens[2]


def start_of(row, lens):
    one, two, three = starts(lens)
    return jnp.where(
        row >= three, three, jnp.where(row >= two, two, jnp.where(row >= one, one, 0))
    )


def prompt_bias(query_dim):
    q = lax.broadcasted_iota(jnp.int32, (PROMPT, PROMPT), query_dim)
    k = lax.broadcasted_iota(jnp.int32, (PROMPT, PROMPT), 1 - query_dim)
    return jnp.where(k <= q, 0.0, -jnp.inf).astype(f32)


def response_bias(lens, query_dim):
    q = lax.broadcasted_iota(jnp.int32, (RESP, RESP), query_dim)
    k = lax.broadcasted_iota(jnp.int32, (RESP, RESP), 1 - query_dim)
    return jnp.where((k <= q) & (k >= start_of(q, lens)), 0.0, -jnp.inf).astype(f32)


def chosen_rows(lens, row_dim):
    dims = (RESP, NRESP * RLEN) if row_dim == 0 else (NRESP * RLEN, RESP)
    row = lax.broadcasted_iota(jnp.int32, dims, row_dim)
    col = lax.broadcasted_iota(jnp.int32, dims, 1 - row_dim)
    one, two, three = starts(lens)
    slot = (
        (row >= one).astype(jnp.int32)
        + (row >= two).astype(jnp.int32)
        + (row >= three).astype(jnp.int32)
    )
    return jnp.where(col == slot * RLEN + row - start_of(row, lens), 1.0, 0.0).astype(bf16)


def pack_kernel(lens, place, x_ref, top_ref, key_ref, value_ref, xp_out, xr_out, tp_out, tr_out, k_out, v_out, chosen):
    @pl.when(pl.program_id(0) == 0)
    def _():
        pick = chosen_rows(lens, 0)
        chosen[...] = pick
        tp_out[...] = top_ref[:PROMPT]
        tr_out[...] = dot(pick, top_ref[PROMPT:]).astype(bf16)
        for ref, out in ((key_ref, k_out), (value_ref, v_out)):
            out[:PROMPT] = ref[:PROMPT]
            out[PROMPT:] = dot(pick, ref[PROMPT:]).astype(bf16)

    live = dot(chosen[...], x_ref[PROMPT:]).astype(bf16)
    for h in range(x_ref.shape[1] // HD):
        cols = slice(h * HD, (h + 1) * HD)
        xp_out[h] = x_ref[:PROMPT, cols]
        xr_out[h] = live[:, cols]


def pack(lens, place, x, top, key, value):
    rows, width = x.shape
    heads = width // HD
    steps = 2
    some = heads // steps
    whole = lambda *dims: pl.BlockSpec(dims, lambda i, l, p: (0,) * len(dims))
    return pl.pallas_call(
        pack_kernel,
        name="pack",
        cost_estimate=about(4),
        grid_spec=pltpu.PrefetchScalarGridSpec(
            num_scalar_prefetch=2,
            grid=(steps,),
            in_specs=[
                pl.BlockSpec((rows, some * HD), lambda i, l, p: (0, i)),
                pl.BlockSpec((rows, HD), lambda i, l, p: (0, p[0])),
                whole(rows, HD),
                whole(rows, HD),
            ],
            out_specs=[
                pl.BlockSpec((some, PROMPT, HD), lambda i, l, p: (i, 0, 0)),
                pl.BlockSpec((some, RESP, HD), lambda i, l, p: (i, 0, 0)),
                whole(PROMPT, HD),
                whole(RESP, HD),
                whole(LIVE, HD),
                whole(LIVE, HD),
            ],
            scratch_shapes=[pltpu.VMEM((RESP, NRESP * RLEN), bf16)],
        ),
        out_shape=[
            shape((heads, PROMPT, HD), bf16),
            shape((heads, RESP, HD), bf16),
            shape((PROMPT, HD), bf16),
            shape((RESP, HD), bf16),
            shape((LIVE, HD), bf16),
            shape((LIVE, HD), bf16),
        ],
        compiler_params=params(60),
    )(lens, place, x, top, key, value)


def softmax(scores, dim):
    top = functools.reduce(jnp.maximum, [jnp.max(x, dim, keepdims=True) for x in scores])
    weights = [jnp.exp2((x - top) * EXP2_SCALE) for x in scores]
    total = functools.reduce(jnp.add, [jnp.sum(w, dim, keepdims=True) for w in weights])
    share = 1.0 / total
    return [w * share for w in weights]


AT_ONCE = 4
PROMPT_ROW = PROMPT + HD
RESP_ROW = 2 * PROMPT + HD
HBM = pl.BlockSpec(memory_space=pl.ANY)
VMEM = pl.BlockSpec(memory_space=pltpu.VMEM)
SMEM = pl.BlockSpec(memory_space=pltpu.SMEM)


def fetch(parts, held, sems):
    rows = held.shape[1]
    return [
        pltpu.make_async_copy(part.at[:, :rows], held.at[SIDE * j : SIDE * (j + 1)], sems.at[j])
        for j, part in enumerate(parts)
    ]


def prob_kernel(prompt, lens, ks, vs, q_ref, *refs):
    k_parts, v_parts = refs[:SIDE], refs[SIDE : 2 * SIDE]
    out, bias, keys, values, k_sems, v_sems = refs[2 * SIDE :]
    i = pl.program_id(0)

    @pl.when(i == 0)
    def _():
        copies = fetch(k_parts, keys, k_sems) + fetch(v_parts, values, v_sems)
        for copy in copies:
            copy.start()
        bias[...] = prompt_bias(0) if prompt else response_bias(lens, 0)
        for copy in copies:
            copy.wait()

    for u in range(AT_ONCE):
        q, k, v = q_ref[u], keys[ks[i * AT_ONCE + u]], values[vs[i * AT_ONCE + u]]
        if prompt:
            (p,) = softmax([dot_nt(q, k) + bias[...]], -1)
            out[u, :, :PROMPT] = p
            out[u, :, PROMPT:] = dot(p.astype(bf16), v)
        else:
            p1, p2 = softmax([dot_nt(q, k[:PROMPT]), dot_nt(q, k[PROMPT:]) + bias[...]], -1)
            out[u, :, :PROMPT] = p1
            out[u, :, PROMPT:LIVE] = p2
            out[u, :, 2 * PROMPT :] = dot(p1.astype(bf16), v[:PROMPT]) + dot(
                p2.astype(bf16), v[PROMPT:]
            )


def prob(prompt, lens, ks, vs, q, k, v):
    n, rows, _ = q.shape
    keys, width = (PROMPT, PROMPT_ROW) if prompt else (LIVE, RESP_ROW)
    block = lambda w: pl.BlockSpec((AT_ONCE, rows, w), lambda i, *tables: (i, 0, 0))
    return pl.pallas_call(
        functools.partial(prob_kernel, prompt),
        name="prompt_prob" if prompt else "response_prob",
        cost_estimate=about(9),
        grid_spec=pltpu.PrefetchScalarGridSpec(
            num_scalar_prefetch=3,
            grid=(n // AT_ONCE,),
            in_specs=[block(HD)] + [HBM] * (2 * SIDE),
            out_specs=block(width),
            scratch_shapes=[
                pltpu.VMEM((rows, rows), f32),
                pltpu.VMEM((n, keys, HD), bf16),
                pltpu.VMEM((n, keys, HD), bf16),
                pltpu.SemaphoreType.DMA((SIDE,)),
                pltpu.SemaphoreType.DMA((SIDE,)),
            ],
        ),
        out_shape=shape((n, rows, width)),
        compiler_params=params(),
    )(lens, ks, vs, q, *k, *v)


GROUPS = ((14, 16), (12, 14), (8, 12), (4, 8), (0, 4))


def chain_kernel(prompt, active, ks, vs, g_in, stash_in, prob_hbm, *refs):
    k_parts, v_parts = refs[:SIDE], refs[SIDE : 2 * SIDE]
    g_out, stash, probs, keys, values, grads, p_sems, k_sems, v_sems, out_sems = refs[2 * SIDE :]

    def load(j):
        span = pl.ds(GROUPS[j][0], GROUPS[j][1] - GROUPS[j][0])
        return pltpu.make_async_copy(prob_hbm.at[span], probs.at[span], p_sems.at[j])

    def save(j):
        span = pl.ds(GROUPS[j][0], GROUPS[j][1] - GROUPS[j][0])
        return pltpu.make_async_copy(grads.at[span], stash.at[span], out_sems.at[j])

    def step(layer):
        d = grads[layer]
        wide = d.astype(f32)
        k, v = keys[ks[layer]], values[vs[layer]]
        if prompt:
            delta = jnp.sum(wide * probs[layer, :, PROMPT:], -1, keepdims=True)
            ds = (probs[layer, :, :PROMPT] * (dot_nt(d, v) - delta)).astype(bf16)
            change = dot(ds, k)
        else:
            delta = jnp.sum(wide * probs[layer, :, 2 * PROMPT :], -1, keepdims=True)
            ds1 = (probs[layer, :, :PROMPT] * (dot_nt(d, v[:PROMPT]) - delta)).astype(bf16)
            ds2 = (probs[layer, :, PROMPT:LIVE] * (dot_nt(d, v[PROMPT:]) - delta)).astype(bf16)
            change = dot(ds1, k[:PROMPT]) + dot(ds2, k[PROMPT:])
        return (wide + change * SCALE).astype(bf16)

    @pl.when(active[0] == 1)
    def _():
        first = fetch(v_parts, values, v_sems) + [load(0)] + fetch(k_parts, keys, k_sems)
        for copy in first:
            copy.start()
        for j in range(1, len(GROUPS)):
            load(j).start()
        grads[GROUPS[0][1] - 1] = g_in[...]
        for copy in first:
            copy.wait()
        for j, (low, high) in enumerate(GROUPS):
            if j:
                load(j).wait()

            def body(i, carry, high=high):
                grads[high - 2 - i] = step(high - 1 - i)
                return carry

            if low:
                lax.fori_loop(0, high - low, body, 0)
            else:
                lax.fori_loop(0, high - 1, body, 0)
                g_out[...] = step(0)
            save(j).start()
        for j in range(len(GROUPS)):
            save(j).wait()


def chain(prompt, active, ks, vs, g, stash, probs, k, v):
    n, rows, width = probs.shape
    count = PROMPT if prompt else LIVE
    return pl.pallas_call(
        functools.partial(chain_kernel, prompt),
        name="prompt_chain" if prompt else "response_chain",
        cost_estimate=about(8),
        in_specs=[SMEM] * 3 + [VMEM] + [HBM] * (2 + 2 * SIDE),
        out_specs=[VMEM, HBM],
        scratch_shapes=[
            pltpu.VMEM((n, rows, width), f32),
            pltpu.VMEM((n, count, HD), bf16),
            pltpu.VMEM((n, count, HD), bf16),
            pltpu.VMEM((n, rows, HD), bf16),
            pltpu.SemaphoreType.DMA((len(GROUPS),)),
            pltpu.SemaphoreType.DMA((SIDE,)),
            pltpu.SemaphoreType.DMA((SIDE,)),
            pltpu.SemaphoreType.DMA((len(GROUPS),)),
        ],
        out_shape=[shape((rows, HD), bf16), shape((n, rows, HD), bf16)],
        input_output_aliases={4: 1},
        compiler_params=params(),
    )(active, ks, vs, g, stash, probs, *k, *v)


HEADS_AT_ONCE = 2


def prompt_grad_kernel(q_ref, g_ref, k_ref, v_ref, out_ref, bias):
    @pl.when(pl.program_id(0) == 0)
    def _():
        bias[...] = prompt_bias(1)
        out_ref[...] = jnp.zeros_like(out_ref)

    k, v = k_ref[...], v_ref[...]
    dk, dv = 0.0, 0.0
    for u in range(HEADS_AT_ONCE):
        q, g = q_ref[u], g_ref[u]
        (p,) = softmax([dot_nt(k, q) + bias[...]], 0)
        dp = dot_nt(v, g)
        pb = p.astype(bf16)
        delta = jnp.sum(pb.astype(f32) * dp, 0, keepdims=True)
        ds = (p * (dp - delta)).astype(bf16)
        dk = dk + dot(ds, q)
        dv = dv + dot(pb, g)
    out_ref[:, :HD] += dk * SCALE
    out_ref[:, HD:] += dv


def prompt_grad(q, g, k, v):
    n = q.shape[0]
    block = pl.BlockSpec((HEADS_AT_ONCE, PROMPT, HD), lambda i: (i, 0, 0))
    whole = lambda w: pl.BlockSpec((PROMPT, w), lambda i: (0, 0))
    return pl.pallas_call(
        prompt_grad_kernel,
        name="prompt_grad",
        cost_estimate=about(8),
        grid=(n // HEADS_AT_ONCE,),
        in_specs=[block, block, whole(HD), whole(HD)],
        out_specs=whole(2 * HD),
        scratch_shapes=[pltpu.VMEM((PROMPT, PROMPT), f32)],
        out_shape=shape((PROMPT, 2 * HD)),
        compiler_params=params(),
    )(q, g, k, v)


def response_grad_kernel(lens, q_ref, g_ref, k_ref, v_ref, part_ref, out_ref, sum_ref, bias, acc):
    i = pl.program_id(0)

    @pl.when(i == 0)
    def _():
        bias[...] = response_bias(lens, 1)
        acc[:PROMPT] = part_ref[...]
        acc[PROMPT:] = jnp.zeros((RESP, 2 * HD), f32)

    k1, k2 = k_ref[:PROMPT], k_ref[PROMPT:]
    v1, v2 = v_ref[:PROMPT], v_ref[PROMPT:]
    dk1, dk2, dv1, dv2 = 0.0, 0.0, 0.0, 0.0
    for u in range(HEADS_AT_ONCE):
        q, g = q_ref[u], g_ref[u]
        p1, p2 = softmax([dot_nt(k1, q), dot_nt(k2, q) + bias[...]], 0)
        dp1, dp2 = dot_nt(v1, g), dot_nt(v2, g)
        pb1, pb2 = p1.astype(bf16), p2.astype(bf16)
        delta = jnp.sum(pb1.astype(f32) * dp1, 0, keepdims=True) + jnp.sum(
            pb2.astype(f32) * dp2, 0, keepdims=True
        )
        ds1 = (p1 * (dp1 - delta)).astype(bf16)
        ds2 = (p2 * (dp2 - delta)).astype(bf16)
        dk1, dk2 = dk1 + dot(ds1, q), dk2 + dot(ds2, q)
        dv1, dv2 = dv1 + dot(pb1, g), dv2 + dot(pb2, g)
    acc[:PROMPT, :HD] += dk1 * SCALE
    acc[PROMPT:, :HD] += dk2 * SCALE
    acc[:PROMPT, HD:] += dv1
    acc[PROMPT:, HD:] += dv2

    @pl.when(i == pl.num_programs(0) - 1)
    def _():
        total = acc[...]
        squares = jnp.sum(total * total, 0, keepdims=True)
        sum_ref[...] = squares[:, :HD] + squares[:, HD:]
        out_ref[:PROMPT] = total[:PROMPT]
        spread = chosen_rows(lens, 1)
        left = total[PROMPT:]
        placed = jnp.zeros((NRESP * RLEN, 2 * HD), f32)
        for _ in range(3):
            term = left.astype(bf16)
            placed = placed + dot(spread, term)
            left = left - term.astype(f32)
        out_ref[PROMPT:] = placed


def response_grad(lens, q, g, k, v, part):
    n = q.shape[0]
    rows = PROMPT + NRESP * RLEN
    block = pl.BlockSpec((HEADS_AT_ONCE, RESP, HD), lambda i, a: (i, 0, 0))
    whole = lambda *dims: pl.BlockSpec(dims, lambda i, a: (0, 0))
    return pl.pallas_call(
        response_grad_kernel,
        name="response_grad",
        cost_estimate=about(11),
        grid_spec=pltpu.PrefetchScalarGridSpec(
            num_scalar_prefetch=1,
            grid=(n // HEADS_AT_ONCE,),
            in_specs=[
                block,
                block,
                whole(LIVE, HD),
                whole(LIVE, HD),
                whole(PROMPT, 2 * HD),
            ],
            out_specs=[whole(rows, 2 * HD), whole(1, HD)],
            scratch_shapes=[pltpu.VMEM((RESP, RESP), f32), pltpu.VMEM((LIVE, 2 * HD), f32)],
        ),
        out_shape=[shape((rows, 2 * HD)), shape((1, HD))],
        compiler_params=params(),
    )(lens, q, g, k, v, part)


def ring(step, size=SIDE):
    return [(i, (i + step) % size) for i in range(size)]


def gathered(block, axis):
    return [block] + [lax.ppermute(block, axis, ring(step)) for step in (1, -1, 2)]


def slot_of(distance):
    distance = distance % SIDE
    return jnp.where(distance == 0, 0, jnp.where(distance == SIDE - 1, 1, distance + 1))


def on_device(hidden_stash, key_stash, value_stash, top_grads, lens):
    stage = lax.axis_index("zl")
    my_x = lax.axis_index("x")
    my_y = lax.axis_index("y")
    place = (my_x * SIDE + my_y).reshape(1).astype(jnp.int32)
    qp, qr, gp, gr, k, v = pack(
        lens, place, hidden_stash[0], top_grads, key_stash[0], value_stash[0]
    )
    layers = jnp.arange(PLANE, dtype=jnp.int32)
    slot_x = slot_of(layers // SIDE - my_x)
    slot_y = slot_of(layers % SIDE - my_y)
    ks = (slot_x * SIDE + slot_y).astype(jnp.int32)
    vs = (slot_y * SIDE + slot_x).astype(jnp.int32)
    plane = ("x", "y")
    swap = lambda a: lax.all_to_all(a, plane, 0, 0, tiled=True)
    row_k = jnp.stack(gathered(k, "y"))
    col_v = jnp.stack(gathered(v, "x"))
    all_k = gathered(row_k, "x")
    all_v = gathered(col_v, "y")
    my_qp = swap(qp)
    my_qr = swap(lax.optimization_barrier((qr, my_qp))[0])
    prob_p = prob(True, lens, ks, vs, my_qp, all_k, all_v)
    prob_r = prob(False, lens, ks, vs, my_qr, all_k, all_v)
    stash_p, stash_r = my_qp, my_qr
    after = lambda x, y: lax.optimization_barrier((x, y))[0]
    for now in range(STAGES - 1, -1, -1):
        active = (stage == now).astype(jnp.int32).reshape(1)
        gp, stash_p = chain(True, active, ks, vs, gp, stash_p, prob_p, all_k, all_v)
        if now:
            sent = lax.ppermute(gp, "zl", [(now, now - 1)])
            gr = after(gr, gp if now == STAGES - 1 else sent)
            gp = sent
        else:
            gr, stash_p = lax.optimization_barrier((gr, stash_p))
        gr, stash_r = chain(False, active, ks, vs, gr, stash_r, prob_r, all_k, all_v)
        if now:
            gp = after(gp, gr)
            gr = lax.ppermute(gr, "zl", [(now, now - 1)])
    part = prompt_grad(after(qp, gr), swap(stash_p), k, v)
    raw, squares = response_grad(lens, qr, swap(stash_r), k, v, part)
    for axes, size in ((plane, PLANE), (("zl", "tp"), STAGES * lax.axis_size("tp"))):
        spread = jnp.broadcast_to(squares, (size, HD))
        squares = jnp.sum(lax.all_to_all(spread, axes, 0, 0, tiled=True), 0, keepdims=True)
    square_sum = jnp.sum(squares)
    entries = STAGES * PLANE * lax.axis_size("tp") * raw.shape[0] * raw.shape[1]
    clip_limit = clip_rms * math.sqrt(entries)
    factor = clip_limit / jnp.maximum(jnp.sqrt(square_sum), clip_limit)
    return (raw * factor)[None]


def solution(mesh):
    parts = mesh.devices.reshape(STAGES, SIDE, SIDE, -1)
    finer = Mesh(parts, ("zl", "x", "y", "tp"))
    pipe = ("zl", "x", "y")
    placed = (
        P(pipe, None, "tp"),
        P(pipe, None, "tp"),
        P(pipe, None, "tp"),
        P(None, "tp"),
        P(),
    )
    return jax.shard_map(
        on_device, mesh=finer, in_specs=placed, out_specs=P(pipe, None, "tp"), check_vma=False
    )
```

```python
import functools
import math

import jax
import jax.numpy as jnp
from jax import lax
from jax.experimental import pallas as pl
from jax.experimental.pallas import tpu as pltpu
from jax.sharding import Mesh, PartitionSpec as P

HD = 128
PROMPT = 256
NRESP = 4
RLEN = 64
RESP = 192
LIVE = PROMPT + RESP
STAGES = 4
SIDE = 4
PLANE = SIDE * SIDE

clip_rms = 0.5
SCALE = 1.0 / math.sqrt(HD)
EXP2_SCALE = SCALE * math.log2(math.e)
f32 = jnp.float32
bf16 = jnp.bfloat16


def dot(a, b):
    return lax.dot_general(a, b, (((1,), (0,)), ((), ())), preferred_element_type=f32)


def dot_nt(a, b):
    return lax.dot_general(a, b, (((1,), (1,)), ((), ())), preferred_element_type=f32)


def about(us):
    return pl.CostEstimate(flops=us * 1_000_000_000, bytes_accessed=0, transcendentals=0)


def params(mebibytes=24):
    return pltpu.CompilerParams(vmem_limit_bytes=mebibytes << 20)


def shape(dims, dtype=f32):
    return jax.ShapeDtypeStruct(dims, dtype)


def starts(lens):
    first = lens[0]
    second = first + lens[1]
    return first, second, second + lens[2]


def start_of(row, lens):
    one, two, three = starts(lens)
    return jnp.where(
        row >= three, three, jnp.where(row >= two, two, jnp.where(row >= one, one, 0))
    )


def prompt_bias(query_dim):
    q = lax.broadcasted_iota(jnp.int32, (PROMPT, PROMPT), query_dim)
    k = lax.broadcasted_iota(jnp.int32, (PROMPT, PROMPT), 1 - query_dim)
    return jnp.where(k <= q, 0.0, -jnp.inf).astype(f32)


def response_bias(lens, query_dim):
    q = lax.broadcasted_iota(jnp.int32, (RESP, RESP), query_dim)
    k = lax.broadcasted_iota(jnp.int32, (RESP, RESP), 1 - query_dim)
    return jnp.where((k <= q) & (k >= start_of(q, lens)), 0.0, -jnp.inf).astype(f32)


def chosen_rows(lens, row_dim):
    dims = (RESP, NRESP * RLEN) if row_dim == 0 else (NRESP * RLEN, RESP)
    row = lax.broadcasted_iota(jnp.int32, dims, row_dim)
    col = lax.broadcasted_iota(jnp.int32, dims, 1 - row_dim)
    one, two, three = starts(lens)
    slot = (
        (row >= one).astype(jnp.int32)
        + (row >= two).astype(jnp.int32)
        + (row >= three).astype(jnp.int32)
    )
    return jnp.where(col == slot * RLEN + row - start_of(row, lens), 1.0, 0.0).astype(bf16)


def pack_kernel(lens, place, x_ref, top_ref, key_ref, value_ref, xp_out, xr_out, tp_out, tr_out, k_out, v_out, chosen):
    @pl.when(pl.program_id(0) == 0)
    def _():
        pick = chosen_rows(lens, 0)
        chosen[...] = pick
        tp_out[...] = top_ref[:PROMPT]
        tr_out[...] = dot(pick, top_ref[PROMPT:]).astype(bf16)
        for ref, out in ((key_ref, k_out), (value_ref, v_out)):
            out[:PROMPT] = ref[:PROMPT]
            out[PROMPT:] = dot(pick, ref[PROMPT:]).astype(bf16)

    live = dot(chosen[...], x_ref[PROMPT:]).astype(bf16)
    for h in range(x_ref.shape[1] // HD):
        cols = slice(h * HD, (h + 1) * HD)
        xp_out[h] = x_ref[:PROMPT, cols]
        xr_out[h] = live[:, cols]


def pack(lens, place, x, top, key, value):
    rows, width = x.shape
    heads = width // HD
    steps = 2
    some = heads // steps
    whole = lambda *dims: pl.BlockSpec(dims, lambda i, l, p: (0,) * len(dims))
    return pl.pallas_call(
        pack_kernel,
        name="pack",
        cost_estimate=about(4),
        grid_spec=pltpu.PrefetchScalarGridSpec(
            num_scalar_prefetch=2,
            grid=(steps,),
            in_specs=[
                pl.BlockSpec((rows, some * HD), lambda i, l, p: (0, i)),
                pl.BlockSpec((rows, HD), lambda i, l, p: (0, p[0])),
                whole(rows, HD),
                whole(rows, HD),
            ],
            out_specs=[
                pl.BlockSpec((some, PROMPT, HD), lambda i, l, p: (i, 0, 0)),
                pl.BlockSpec((some, RESP, HD), lambda i, l, p: (i, 0, 0)),
                whole(PROMPT, HD),
                whole(RESP, HD),
                whole(LIVE, HD),
                whole(LIVE, HD),
            ],
            scratch_shapes=[pltpu.VMEM((RESP, NRESP * RLEN), bf16)],
        ),
        out_shape=[
            shape((heads, PROMPT, HD), bf16),
            shape((heads, RESP, HD), bf16),
            shape((PROMPT, HD), bf16),
            shape((RESP, HD), bf16),
            shape((LIVE, HD), bf16),
            shape((LIVE, HD), bf16),
        ],
        compiler_params=params(60),
    )(lens, place, x, top, key, value)


def softmax(scores, dim):
    top = functools.reduce(jnp.maximum, [jnp.max(x, dim, keepdims=True) for x in scores])
    weights = [jnp.exp2((x - top) * EXP2_SCALE) for x in scores]
    total = functools.reduce(jnp.add, [jnp.sum(w, dim, keepdims=True) for w in weights])
    share = 1.0 / total
    return [w * share for w in weights]


AT_ONCE = 4
PROMPT_ROW = PROMPT + HD
RESP_ROW = 2 * PROMPT + HD
VMEM = pl.BlockSpec(memory_space=pltpu.VMEM)
SMEM = pl.BlockSpec(memory_space=pltpu.SMEM)
HBM = pl.BlockSpec(memory_space=pltpu.HBM)


def kept(x):
    return pltpu.with_memory_space_constraint(x, pltpu.VMEM)


def in_hbm(x):
    return pltpu.with_memory_space_constraint(x, pltpu.HBM)


def prob_kernel(prompt, lens, k_from, v_from, q_ref, *refs):
    half = (len(refs) - 9) // 2
    k_parts, v_parts = refs[:half], refs[half : 2 * half]
    probs_out, keys_out, values_out, probs, keys, values, bias, sems, kv_sems = refs[2 * half :]
    n, count, _ = keys.shape
    bias[...] = prompt_bias(0) if prompt else response_bias(lens, 0)
    for parts, held, table in ((k_parts, keys, k_from), (v_parts, values, v_from)):
        at = 0
        for part in parts:
            for i in range(part.shape[0]):
                held[table[at]] = part[i, :count]
                at += 1
    ordered = [
        pltpu.make_async_copy(held, out, kv_sems.at[j])
        for j, (held, out) in enumerate(((keys, keys_out), (values, values_out)))
    ]
    for copy in ordered:
        copy.start()

    def done(i):
        some = pl.ds(i * AT_ONCE, AT_ONCE)
        return pltpu.make_async_copy(probs.at[some], probs_out.at[some], sems.at[i])

    def body(i, carry):
        for u in range(AT_ONCE):
            layer = i * AT_ONCE + u
            q, k, v = q_ref[layer], keys[layer], values[layer]
            if prompt:
                (p,) = softmax([dot_nt(q, k) + bias[...]], -1)
                probs[layer, :, :PROMPT] = p
                probs[layer, :, PROMPT:] = dot(p.astype(bf16), v)
            else:
                p1, p2 = softmax([dot_nt(q, k[:PROMPT]), dot_nt(q, k[PROMPT:]) + bias[...]], -1)
                probs[layer, :, :PROMPT] = p1
                probs[layer, :, PROMPT:LIVE] = p2
                probs[layer, :, 2 * PROMPT :] = dot(p1.astype(bf16), v[:PROMPT]) + dot(
                    p2.astype(bf16), v[PROMPT:]
                )
        done(i).start()
        return carry

    lax.fori_loop(0, n // AT_ONCE, body, 0)
    for copy in ordered + [done(i) for i in range(n // AT_ONCE)]:
        copy.wait()


def prob(prompt, lens, k_from, v_from, q, k, v):
    n, rows, _ = q.shape
    count, width = (PROMPT, PROMPT_ROW) if prompt else (LIVE, RESP_ROW)
    results = [((n, rows, width), f32), ((n, count, HD), bf16), ((n, count, HD), bf16)]
    return pl.pallas_call(
        functools.partial(prob_kernel, prompt),
        name="prompt_prob" if prompt else "response_prob",
        cost_estimate=about(7),
        in_specs=[SMEM] * 3 + [VMEM] * (1 + len(k) + len(v)),
        out_specs=[HBM] * 3,
        scratch_shapes=[pltpu.VMEM(*r) for r in results]
        + [
            pltpu.VMEM((rows, rows), f32),
            pltpu.SemaphoreType.DMA((n // AT_ONCE,)),
            pltpu.SemaphoreType.DMA((2,)),
        ],
        out_shape=[pltpu.HBM(*r) for r in results],
        compiler_params=params(22),
    )(lens, k_from, v_from, q, *k, *v)


GROUPS = ((15, 16), (14, 15), (12, 14), (8, 12), (4, 8), (0, 4))
AHEAD = 3


def chain_kernel(prompt, active, g_in, stash_in, probs_in, keys_in, values_in, g_out, stash, probs, keys, values, grads, sems, save_sems):
    n = keys.shape[0]

    def loads(j):
        span = pl.ds(GROUPS[j][0], GROUPS[j][1] - GROUPS[j][0])
        return [
            pltpu.make_async_copy(source.at[span], held.at[span], sems.at[j, i])
            for i, (source, held) in enumerate(
                ((values_in, values), (probs_in, probs), (keys_in, keys))
            )
        ]

    def step(layer):
        d = grads[layer]
        wide = d.astype(f32)
        k, v = keys[layer], values[layer]
        if prompt:
            delta = jnp.sum(wide * probs[layer, :, PROMPT:], -1, keepdims=True)
            ds = (probs[layer, :, :PROMPT] * (dot_nt(d, v) - delta)).astype(bf16)
            change = dot(ds, k)
        else:
            delta = jnp.sum(wide * probs[layer, :, 2 * PROMPT :], -1, keepdims=True)
            ds1 = (probs[layer, :, :PROMPT] * (dot_nt(d, v[:PROMPT]) - delta)).astype(bf16)
            ds2 = (probs[layer, :, PROMPT:LIVE] * (dot_nt(d, v[PROMPT:]) - delta)).astype(bf16)
            change = dot(ds1, k[:PROMPT]) + dot(ds2, k[PROMPT:])
        return (wide + change * SCALE).astype(bf16)

    def save(j):
        half = pl.ds(j * n // 2, n // 2)
        return pltpu.make_async_copy(grads.at[half], stash.at[half], save_sems.at[j])

    @pl.when(active[0] == 1)
    def _():
        for j in range(AHEAD):
            for copy in loads(j):
                copy.start()
        grads[n - 1] = g_in[...]
        for j, (low, high) in enumerate(GROUPS):
            for copy in loads(j):
                copy.wait()
            if j + AHEAD < len(GROUPS):
                for copy in loads(j + AHEAD):
                    copy.start()

            def body(i, carry, high=high):
                grads[high - 2 - i] = step(high - 1 - i)
                return carry

            if high - low == 1:
                body(0, 0)
            else:
                lax.fori_loop(0, high - max(low, 1), body, 0)
            if low == n // 2:
                save(1).start()
        save(0).start()
        g_out[...] = step(0)
        save(1).wait()
        save(0).wait()


def chain(prompt, active, g, stash, probs, k, v):
    n, rows, _ = probs.shape
    anywhere = pl.BlockSpec(memory_space=pl.ANY)
    return pl.pallas_call(
        functools.partial(chain_kernel, prompt),
        name="prompt_chain" if prompt else "response_chain",
        cost_estimate=about(7),
        in_specs=[SMEM, VMEM, anywhere] + [HBM] * 3,
        out_specs=[VMEM, anywhere],
        scratch_shapes=[
            pltpu.VMEM(probs.shape, f32),
            pltpu.VMEM(k.shape, bf16),
            pltpu.VMEM(v.shape, bf16),
            pltpu.VMEM((n, rows, HD), bf16),
            pltpu.SemaphoreType.DMA((len(GROUPS), 3)),
            pltpu.SemaphoreType.DMA((2,)),
        ],
        out_shape=[shape((rows, HD), bf16), shape((n, rows, HD), bf16)],
        input_output_aliases={2: 1},
        compiler_params=params(22),
    )(active, g, stash, in_hbm(probs), in_hbm(k), in_hbm(v))


HEADS_AT_ONCE = 2


def own_prob_kernel(prompt, lens, q_ref, k_ref, probs, bias):
    bias[...] = prompt_bias(1) if prompt else response_bias(lens, 1)
    k1, k2 = k_ref[:PROMPT], k_ref[PROMPT:]

    def body(i, carry):
        for u in range(AT_ONCE):
            head = i * AT_ONCE + u
            q = q_ref[head]
            if prompt:
                (probs[head],) = softmax([dot_nt(k1, q) + bias[...]], 0)
            else:
                p1, p2 = softmax([dot_nt(k1, q), dot_nt(k2, q) + bias[...]], 0)
                probs[head, :PROMPT] = p1
                probs[head, PROMPT:] = p2
        return carry

    lax.fori_loop(0, q_ref.shape[0] // AT_ONCE, body, 0)


def own_prob(prompt, lens, q, k):
    n, rows, _ = q.shape
    return pl.pallas_call(
        functools.partial(own_prob_kernel, prompt),
        name="own_prompt_prob" if prompt else "own_response_prob",
        cost_estimate=about(5),
        in_specs=[SMEM, VMEM, VMEM],
        out_specs=VMEM,
        scratch_shapes=[pltpu.VMEM((rows, rows), f32)],
        out_shape=pltpu.VMEM((n, PROMPT if prompt else LIVE, rows), f32),
        compiler_params=params(12),
    )(lens, q, k)


def response_grad_kernel(lens, probs, q_ref, g_ref, v_ref, prompt_out, out_ref, sum_ref, acc):
    acc[...] = jnp.zeros_like(acc)
    v1, v2 = v_ref[:PROMPT], v_ref[PROMPT:]

    def body(i, carry):
        dk1, dk2, dv1, dv2 = 0.0, 0.0, 0.0, 0.0
        for u in range(HEADS_AT_ONCE):
            head = i * HEADS_AT_ONCE + u
            q, g = q_ref[head], g_ref[head]
            p1, p2 = probs[head, :PROMPT], probs[head, PROMPT:]
            dp1, dp2 = dot_nt(v1, g), dot_nt(v2, g)
            pb1, pb2 = p1.astype(bf16), p2.astype(bf16)
            delta = jnp.sum(pb1.astype(f32) * dp1, 0, keepdims=True) + jnp.sum(
                pb2.astype(f32) * dp2, 0, keepdims=True
            )
            ds1 = (p1 * (dp1 - delta)).astype(bf16)
            ds2 = (p2 * (dp2 - delta)).astype(bf16)
            dk1, dk2 = dk1 + dot(ds1, q), dk2 + dot(ds2, q)
            dv1, dv2 = dv1 + dot(pb1, g), dv2 + dot(pb2, g)
        acc[:PROMPT, :HD] += dk1 * SCALE
        acc[PROMPT:, :HD] += dk2 * SCALE
        acc[:PROMPT, HD:] += dv1
        acc[PROMPT:, HD:] += dv2
        return carry

    lax.fori_loop(0, q_ref.shape[0] // HEADS_AT_ONCE, body, 0)
    prompt_out[...] = acc[:PROMPT]
    left = acc[PROMPT:]
    squares = jnp.sum(left * left, 0, keepdims=True)
    sum_ref[...] = squares[:, :HD] + squares[:, HD:]
    spread = chosen_rows(lens, 1)
    placed = jnp.zeros((NRESP * RLEN, 2 * HD), f32)
    for _ in range(3):
        term = left.astype(bf16)
        placed = placed + dot(spread, term)
        left = left - term.astype(f32)
    out_ref[...] = placed


def response_grad(lens, probs, q, g, v):
    return pl.pallas_call(
        response_grad_kernel,
        name="response_grad",
        cost_estimate=about(8),
        in_specs=[SMEM] + [VMEM] * 4,
        out_specs=[VMEM] * 3,
        scratch_shapes=[pltpu.VMEM((LIVE, 2 * HD), f32)],
        out_shape=[shape((PROMPT, 2 * HD)), shape((NRESP * RLEN, 2 * HD)), shape((1, HD))],
        compiler_params=params(12),
    )(lens, kept(probs), q, g, v)


def prompt_grad_kernel(probs, q_ref, g_ref, v_ref, part_ref, response_ref, squares_ref, out_ref, sum_ref, acc):
    acc[...] = part_ref[...]
    v = v_ref[:PROMPT]

    def body(i, carry):
        dk, dv = 0.0, 0.0
        for u in range(HEADS_AT_ONCE):
            head = i * HEADS_AT_ONCE + u
            q, g, p = q_ref[head], g_ref[head], probs[head]
            dp = dot_nt(v, g)
            pb = p.astype(bf16)
            delta = jnp.sum(pb.astype(f32) * dp, 0, keepdims=True)
            ds = (p * (dp - delta)).astype(bf16)
            dk = dk + dot(ds, q)
            dv = dv + dot(pb, g)
        acc[:, :HD] += dk * SCALE
        acc[:, HD:] += dv
        return carry

    lax.fori_loop(0, q_ref.shape[0] // HEADS_AT_ONCE, body, 0)
    total = acc[...]
    squares = jnp.sum(total * total, 0, keepdims=True)
    sum_ref[...] = squares_ref[...] + squares[:, :HD] + squares[:, HD:]
    out_ref[:PROMPT] = total
    out_ref[PROMPT:] = response_ref[...]


def prompt_grad(probs, q, g, v, part, response, squares):
    return pl.pallas_call(
        prompt_grad_kernel,
        name="prompt_grad",
        cost_estimate=about(5),
        in_specs=[VMEM] * 7,
        out_specs=[VMEM] * 2,
        scratch_shapes=[pltpu.VMEM((PROMPT, 2 * HD), f32)],
        out_shape=[shape((PROMPT + NRESP * RLEN, 2 * HD)), shape((1, HD))],
        compiler_params=params(12),
    )(kept(probs), q, g, v, part, response, squares)


def ring(step, size=SIDE):
    return [(i, (i + step) % size) for i in range(size)]


def gathered(block, axis):
    return [block] + [lax.ppermute(block, axis, ring(step)) for step in (1, -1, 2)]


def gathered_halves(block, axis):
    low, high = (lax.ppermute(block, axis, ring(step)) for step in (1, -1))
    half = block.shape[0] // 2
    return [
        block,
        low,
        high,
        lax.ppermute(low[:half], axis, ring(1)),
        lax.ppermute(high[half:], axis, ring(-1)),
    ]


def on_device(hidden_stash, key_stash, value_stash, top_grads, lens):
    stage = lax.axis_index("zl")
    my_x = lax.axis_index("x")
    my_y = lax.axis_index("y")
    place = (my_x * SIDE + my_y).reshape(1).astype(jnp.int32)
    qp, qr, gp, gr, k, v = pack(
        lens, place, hidden_stash[0], top_grads, key_stash[0], value_stash[0]
    )
    parts = jnp.arange(PLANE, dtype=jnp.int32)
    away = lambda slot: jnp.where(slot == 1, 3, jnp.where(slot == 2, 1, jnp.where(slot == 3, 2, 0)))
    outer, inner = away(parts // SIDE), away(parts % SIDE)
    k_from = ((my_x + outer) % SIDE * SIDE + (my_y + inner) % SIDE).astype(jnp.int32)
    v_from = ((my_x + inner) % SIDE * SIDE + (my_y + outer) % SIDE).astype(jnp.int32)
    plane = ("x", "y")
    swap = lambda a: lax.all_to_all(a, plane, 0, 0, tiled=True)
    after = lambda x, y: lax.optimization_barrier((x, y))[0]
    row_k = jnp.stack(gathered(k, "y"))
    col_v = jnp.stack(gathered(v, "x"))
    row_k, col_v, qp = lax.optimization_barrier((row_k, col_v, qp))
    my_qp = swap(qp)
    all_k = gathered_halves(row_k, "x")
    all_v = gathered_halves(col_v, "y")
    my_qr = swap(after(qr, my_qp))
    prob_p, key_p, value_p = prob(True, lens, k_from, v_from, my_qp, all_k, all_v)
    prob_r, key_r, value_r = prob(False, lens, k_from, v_from, my_qr, all_k, all_v)
    stash_p, stash_r = my_qp, my_qr
    for now in range(STAGES - 1, -1, -1):
        active = (stage == now).astype(jnp.int32).reshape(1)
        gp, stash_p = chain(True, active, gp, stash_p, prob_p, key_p, value_p)
        if now:
            sent = lax.ppermute(gp, "zl", [(now, now - 1)])
            gr = after(gr, gp if now == STAGES - 1 else sent)
            gp = sent
        else:
            gr, stash_p = lax.optimization_barrier((gr, stash_p))
        gr, stash_r = chain(False, active, gr, stash_r, prob_r, key_r, value_r)
        if now:
            gp = after(gp, gr)
            gr = lax.ppermute(gr, "zl", [(now, now - 1)])
    own_gr, own_gp = swap(stash_r), swap(after(stash_p, gr))
    qp, qr = after(qp, gr), after(qr, gr)
    own_r = own_prob(False, lens, qr, k)
    part, response, squares = response_grad(lens, own_r, qr, own_gr, v)
    own_p = own_prob(True, lens, qp, k)
    raw, squares = prompt_grad(own_p, qp, own_gp, v, part, response, squares)
    for axes, size in ((plane, PLANE), (("zl", "tp"), STAGES * lax.axis_size("tp"))):
        spread = jnp.broadcast_to(squares, (size, HD))
        squares = jnp.sum(lax.all_to_all(spread, axes, 0, 0, tiled=True), 0, keepdims=True)
    square_sum = jnp.sum(squares)
    entries = STAGES * PLANE * lax.axis_size("tp") * raw.shape[0] * raw.shape[1]
    clip_limit = clip_rms * math.sqrt(entries)
    factor = clip_limit / jnp.maximum(jnp.sqrt(square_sum), clip_limit)
    return (raw * factor)[None]


def solution(mesh):
    parts = mesh.devices.reshape(STAGES, SIDE, SIDE, -1)
    finer = Mesh(parts, ("zl", "x", "y", "tp"))
    pipe = ("zl", "x", "y")
    placed = (
        P(pipe, None, "tp"),
        P(pipe, None, "tp"),
        P(pipe, None, "tp"),
        P(None, "tp"),
        P(),
    )
    return jax.shard_map(
        on_device, mesh=finer, in_specs=placed, out_specs=P(pipe, None, "tp"), check_vma=False
    )
```

```python
import functools
import math

import jax
import jax.numpy as jnp
from jax import lax
from jax.experimental import pallas as pl
from jax.experimental.pallas import tpu as pltpu
from jax.sharding import Mesh, PartitionSpec as P

HD = 128
PROMPT = 256
NRESP = 4
RLEN = 64
RESP = 192
LIVE = PROMPT + RESP
STAGES = 4
SIDE = 4
PLANE = SIDE * SIDE

clip_rms = 0.5
SCALE = 1.0 / math.sqrt(HD)
EXP2_SCALE = SCALE * math.log2(math.e)
f32 = jnp.float32
bf16 = jnp.bfloat16


VMEM = pl.BlockSpec(memory_space=pltpu.VMEM)
SMEM = pl.BlockSpec(memory_space=pltpu.SMEM)
HBM = pl.BlockSpec(memory_space=pltpu.HBM)


def dot(a, b):
    return lax.dot_general(a, b, (((1,), (0,)), ((), ())), preferred_element_type=f32)


def dot_nt(a, b):
    return lax.dot_general(a, b, (((1,), (1,)), ((), ())), preferred_element_type=f32)


def about(us):
    return pl.CostEstimate(flops=us * 1_000_000_000, bytes_accessed=0, transcendentals=0)


def params(mebibytes=24):
    return pltpu.CompilerParams(vmem_limit_bytes=mebibytes << 20)


def shape(dims, dtype=f32):
    return jax.ShapeDtypeStruct(dims, dtype)


def starts(lens):
    first = lens[0]
    second = first + lens[1]
    return first, second, second + lens[2]


def start_of(row, lens):
    one, two, three = starts(lens)
    return jnp.where(
        row >= three, three, jnp.where(row >= two, two, jnp.where(row >= one, one, 0))
    )


def prompt_bias(query_dim):
    q = lax.broadcasted_iota(jnp.int32, (PROMPT, PROMPT), query_dim)
    k = lax.broadcasted_iota(jnp.int32, (PROMPT, PROMPT), 1 - query_dim)
    return jnp.where(k <= q, 0.0, -jnp.inf).astype(f32)


def response_bias(lens, query_dim, repeats=1):
    dims = (RESP, repeats * RESP)
    q = lax.broadcasted_iota(jnp.int32, dims, query_dim)
    k = lax.broadcasted_iota(jnp.int32, dims, 1 - query_dim)
    for _ in range(repeats - 1):
        q = jnp.where(q >= RESP, q - RESP, q)
    return jnp.where((k <= q) & (k >= start_of(q, lens)), 0.0, -jnp.inf).astype(f32)


def chosen_rows(lens, row_dim):
    dims = (RESP, NRESP * RLEN) if row_dim == 0 else (NRESP * RLEN, RESP)
    row = lax.broadcasted_iota(jnp.int32, dims, row_dim)
    col = lax.broadcasted_iota(jnp.int32, dims, 1 - row_dim)
    one, two, three = starts(lens)
    slot = (
        (row >= one).astype(jnp.int32)
        + (row >= two).astype(jnp.int32)
        + (row >= three).astype(jnp.int32)
    )
    return jnp.where(col == slot * RLEN + row - start_of(row, lens), 1.0, 0.0).astype(bf16)


def pack_kernel(lens, place, x_ref, top_ref, xp_out, xr_out, tp_out, tr_out, chosen):
    @pl.when(pl.program_id(0) == 0)
    def _():
        pick = chosen_rows(lens, 0)
        chosen[...] = pick
        tp_out[...] = top_ref[:PROMPT]
        tr_out[...] = dot(pick, top_ref[PROMPT:]).astype(bf16)

    live = dot(chosen[...], x_ref[PROMPT:]).astype(bf16)
    for h in range(x_ref.shape[1] // HD):
        cols = slice(h * HD, (h + 1) * HD)
        xp_out[h] = x_ref[:PROMPT, cols]
        xr_out[h] = live[:, cols]


def pack(lens, place, x, top):
    rows, width = x.shape
    heads = width // HD
    steps = 2
    some = heads // steps
    whole = lambda n: pl.BlockSpec((n, HD), lambda i, l, p: (0, 0))
    return pl.pallas_call(
        pack_kernel,
        name="pack",
        cost_estimate=about(4),
        grid_spec=pltpu.PrefetchScalarGridSpec(
            num_scalar_prefetch=2,
            grid=(steps,),
            in_specs=[
                pl.BlockSpec((rows, some * HD), lambda i, l, p: (0, i)),
                pl.BlockSpec((rows, HD), lambda i, l, p: (0, p[0])),
            ],
            out_specs=[
                pl.BlockSpec((some, PROMPT, HD), lambda i, l, p: (i, 0, 0)),
                pl.BlockSpec((some, RESP, HD), lambda i, l, p: (i, 0, 0)),
                whole(PROMPT),
                whole(RESP),
            ],
            scratch_shapes=[pltpu.VMEM((RESP, NRESP * RLEN), bf16)],
        ),
        out_shape=[
            shape((heads, PROMPT, HD), bf16),
            shape((heads, RESP, HD), bf16),
            shape((PROMPT, HD), bf16),
            shape((RESP, HD), bf16),
        ],
        compiler_params=params(60),
    )(lens, place, x, top)


def stack_live_kernel(lens, *refs):
    out_k, out_v = refs[2 * SIDE :]
    chosen = chosen_rows(lens, 0)
    for parts, out in ((refs[:SIDE], out_k), (refs[SIDE : 2 * SIDE], out_v)):
        for i, part in enumerate(parts):
            out[i, :PROMPT] = part[:PROMPT]
            out[i, PROMPT:] = dot(chosen, part[PROMPT:]).astype(bf16)


def stack_live(lens, keys, values):
    return pl.pallas_call(
        stack_live_kernel,
        name="stack_live",
        cost_estimate=about(2),
        in_specs=[SMEM] + [VMEM] * (2 * SIDE),
        out_specs=[VMEM] * 2,
        out_shape=[shape((SIDE, LIVE, HD), bf16)] * 2,
        compiler_params=params(8),
    )(lens, *keys, *values)


def softmax(scores, dim):
    top = functools.reduce(jnp.maximum, [jnp.max(x, dim, keepdims=True) for x in scores])
    weights = [jnp.exp2((x - top) * EXP2_SCALE) for x in scores]
    total = functools.reduce(jnp.add, [jnp.sum(w, dim, keepdims=True) for w in weights])
    share = 1.0 / total
    return [w * share for w in weights]


AT_ONCE = 4
PROMPT_ROW = PROMPT + HD
RESP_ROW = 2 * PROMPT + HD
def in_hbm(x):
    return pltpu.with_memory_space_constraint(x, pltpu.HBM)


def prob_kernel(prompt, lens, k_from, v_from, q_ref, *refs):
    half = (len(refs) - 9) // 2
    k_parts, v_parts = refs[:half], refs[half : 2 * half]
    probs_out, keys_out, values_out, probs, keys, values, bias, sems, kv_sems = refs[2 * half :]
    n, count, _ = keys.shape
    bias[...] = prompt_bias(0) if prompt else response_bias(lens, 0)
    for parts, held, table in ((k_parts, keys, k_from), (v_parts, values, v_from)):
        at = 0
        for part in parts:
            for i in range(part.shape[0]):
                held[table[at]] = part[i, :count]
                at += 1
    ordered = [
        pltpu.make_async_copy(held, out, kv_sems.at[j])
        for j, (held, out) in enumerate(((keys, keys_out), (values, values_out)))
    ]
    for copy in ordered:
        copy.start()

    def done(i):
        some = pl.ds(i * AT_ONCE, AT_ONCE)
        return pltpu.make_async_copy(probs.at[some], probs_out.at[some], sems.at[i])

    def body(i, carry):
        for u in range(AT_ONCE):
            layer = i * AT_ONCE + u
            q, k, v = q_ref[layer], keys[layer], values[layer]
            if prompt:
                (p,) = softmax([dot_nt(q, k) + bias[...]], -1)
                probs[layer, :, :PROMPT] = p
                probs[layer, :, PROMPT:] = dot(p.astype(bf16), v)
            else:
                p1, p2 = softmax([dot_nt(q, k[:PROMPT]), dot_nt(q, k[PROMPT:]) + bias[...]], -1)
                probs[layer, :, :PROMPT] = p1
                probs[layer, :, PROMPT:LIVE] = p2
                probs[layer, :, 2 * PROMPT :] = dot(p1.astype(bf16), v[:PROMPT]) + dot(
                    p2.astype(bf16), v[PROMPT:]
                )
        done(i).start()
        return carry

    lax.fori_loop(0, n // AT_ONCE, body, 0)
    for copy in ordered + [done(i) for i in range(n // AT_ONCE)]:
        copy.wait()


def prob(prompt, lens, k_from, v_from, q, k, v):
    n, rows, _ = q.shape
    count, width = (PROMPT, PROMPT_ROW) if prompt else (LIVE, RESP_ROW)
    results = [((n, rows, width), f32), ((n, count, HD), bf16), ((n, count, HD), bf16)]
    return pl.pallas_call(
        functools.partial(prob_kernel, prompt),
        name="prompt_prob" if prompt else "response_prob",
        cost_estimate=about(7),
        in_specs=[SMEM] * 3 + [VMEM] * (1 + len(k) + len(v)),
        out_specs=[HBM] * 3,
        scratch_shapes=[pltpu.VMEM(*r) for r in results]
        + [
            pltpu.VMEM((rows, rows), f32),
            pltpu.SemaphoreType.DMA((n // AT_ONCE,)),
            pltpu.SemaphoreType.DMA((2,)),
        ],
        out_shape=[pltpu.HBM(*r) for r in results],
        compiler_params=params(22),
    )(lens, k_from, v_from, q, *k, *v)


GROUPS = ((15, 16), (14, 15), (12, 14), (8, 12), (4, 8), (0, 4))
AHEAD = 3


def chain_kernel(prompt, active, g_in, stash_in, probs_in, keys_in, values_in, g_out, stash, probs, keys, values, grads, sems, save_sems):
    n = keys.shape[0]

    def loads(j):
        span = pl.ds(GROUPS[j][0], GROUPS[j][1] - GROUPS[j][0])
        return [
            pltpu.make_async_copy(source.at[span], held.at[span], sems.at[j, i])
            for i, (source, held) in enumerate(
                ((values_in, values), (probs_in, probs), (keys_in, keys))
            )
        ]

    def step(layer):
        d = grads[layer]
        wide = d.astype(f32)
        k, v = keys[layer], values[layer]
        if prompt:
            delta = jnp.sum(wide * probs[layer, :, PROMPT:], -1, keepdims=True)
            ds = (probs[layer, :, :PROMPT] * (dot_nt(d, v) - delta)).astype(bf16)
            change = dot(ds, k)
        else:
            delta = jnp.sum(wide * probs[layer, :, 2 * PROMPT :], -1, keepdims=True)
            ds1 = (probs[layer, :, :PROMPT] * (dot_nt(d, v[:PROMPT]) - delta)).astype(bf16)
            ds2 = (probs[layer, :, PROMPT:LIVE] * (dot_nt(d, v[PROMPT:]) - delta)).astype(bf16)
            change = dot(ds1, k[:PROMPT]) + dot(ds2, k[PROMPT:])
        return (wide + change * SCALE).astype(bf16)

    def save(j):
        half = pl.ds(j * n // 2, n // 2)
        return pltpu.make_async_copy(grads.at[half], stash.at[half], save_sems.at[j])

    @pl.when(active[0] == 1)
    def _():
        for j in range(AHEAD):
            for copy in loads(j):
                copy.start()
        grads[n - 1] = g_in[...]
        for j, (low, high) in enumerate(GROUPS):
            for copy in loads(j):
                copy.wait()
            if j + AHEAD < len(GROUPS):
                for copy in loads(j + AHEAD):
                    copy.start()

            def body(i, carry, high=high):
                grads[high - 2 - i] = step(high - 1 - i)
                return carry

            if high - low == 1:
                body(0, 0)
            else:
                lax.fori_loop(0, high - max(low, 1), body, 0)
            if low == n // 2:
                save(1).start()
        save(0).start()
        g_out[...] = step(0)
        save(1).wait()
        save(0).wait()


def chain(prompt, active, g, stash, probs, k, v):
    n, rows, _ = probs.shape
    anywhere = pl.BlockSpec(memory_space=pl.ANY)
    return pl.pallas_call(
        functools.partial(chain_kernel, prompt),
        name="prompt_chain" if prompt else "response_chain",
        cost_estimate=about(7),
        in_specs=[SMEM, VMEM, anywhere] + [HBM] * 3,
        out_specs=[VMEM, anywhere],
        scratch_shapes=[
            pltpu.VMEM(probs.shape, f32),
            pltpu.VMEM(k.shape, bf16),
            pltpu.VMEM(v.shape, bf16),
            pltpu.VMEM((n, rows, HD), bf16),
            pltpu.SemaphoreType.DMA((len(GROUPS), 3)),
            pltpu.SemaphoreType.DMA((2,)),
        ],
        out_shape=[shape((rows, HD), bf16), shape((n, rows, HD), bf16)],
        input_output_aliases={2: 1},
        compiler_params=params(22),
    )(active, g, stash, in_hbm(probs), in_hbm(k), in_hbm(v))


HEADS_AT_ONCE = 2


def own_prob_kernel(prompt, active, lens, q_ref, k_ref, *refs):
    out, probs, queries, bias, sems, q_sem = refs[-6:]
    steps = queries.shape[0] // AT_ONCE

    def done(i):
        some = pl.ds(i * AT_ONCE, AT_ONCE) if prompt else pl.ds(i, 1)
        return pltpu.make_async_copy(probs.at[some], out.at[some], sems.at[i])

    @pl.when(active[0] == 1)
    def _():
        fetch = pltpu.make_async_copy(q_ref, queries, q_sem)
        fetch.start()
        if prompt:
            bias[...] = prompt_bias(1)
        else:
            bias[...] = response_bias(lens, 1, AT_ONCE)
        k1, k2 = k_ref[:PROMPT], k_ref[PROMPT:]
        fetch.wait()

        def body(i, carry):
            if prompt:
                for u in range(AT_ONCE):
                    head = i * AT_ONCE + u
                    (probs[head],) = softmax([dot_nt(k1, queries[head]) + bias[...]], 0)
            else:
                q = queries[pl.ds(i * AT_ONCE, AT_ONCE)].reshape(AT_ONCE * RESP, HD)
                p1, p2 = softmax([dot_nt(k1, q), dot_nt(k2, q) + bias[...]], 0)
                probs[i, :PROMPT] = p1
                probs[i, PROMPT:] = p2
            done(i).start()
            return carry

        lax.fori_loop(0, steps, body, 0)
        for i in range(steps):
            done(i).wait()


def own_prob(prompt, active, lens, q, k, earlier=None, us=5):
    n, rows, _ = q.shape
    dims = (n, PROMPT, rows) if prompt else (n // AT_ONCE, LIVE, AT_ONCE * RESP)
    more = [] if earlier is None else [in_hbm(earlier)]
    return pl.pallas_call(
        functools.partial(own_prob_kernel, prompt),
        name="own_prompt_prob" if prompt else "own_response_prob",
        cost_estimate=about(us),
        in_specs=[SMEM, SMEM, HBM, VMEM] + [HBM] * len(more),
        out_specs=HBM,
        scratch_shapes=[
            pltpu.VMEM(dims, f32),
            pltpu.VMEM(q.shape, bf16),
            pltpu.VMEM((rows, rows if prompt else AT_ONCE * RESP), f32),
            pltpu.SemaphoreType.DMA((n // AT_ONCE,)),
            pltpu.SemaphoreType.DMA,
        ],
        out_shape=pltpu.HBM(dims, f32),
        input_output_aliases={4: 0} if more else {},
        compiler_params=params(16),
    )(active, lens, in_hbm(q), k, *more)


def prompt_grad_kernel(probs, q_ref, g_ref, v_ref, out_ref):
    @pl.when(pl.program_id(0) == 0)
    def _():
        out_ref[...] = jnp.zeros_like(out_ref)

    v = v_ref[...]

    def body(j, carry):
        dk, dv = 0.0, 0.0
        for i in range(HEADS_AT_ONCE):
            u = j * HEADS_AT_ONCE + i
            q, g, p = q_ref[u], g_ref[u], probs[u]
            dp = dot_nt(v, g)
            pb = p.astype(bf16)
            delta = jnp.sum(pb.astype(f32) * dp, 0, keepdims=True)
            ds = (p * (dp - delta)).astype(bf16)
            dk = dk + dot(ds, q)
            dv = dv + dot(pb, g)
        out_ref[:, :HD] += dk * SCALE
        out_ref[:, HD:] += dv
        return carry

    lax.fori_loop(0, q_ref.shape[0] // HEADS_AT_ONCE, body, 0)


def prompt_grad(probs, q, g, v):
    n = q.shape[0]
    block = lambda *dims: pl.BlockSpec((AT_ONCE,) + dims, lambda i: (i, 0, 0))
    whole = lambda *dims: pl.BlockSpec(dims, lambda i: (0, 0))
    return pl.pallas_call(
        prompt_grad_kernel,
        name="prompt_grad",
        cost_estimate=about(5),
        grid=(n // AT_ONCE,),
        in_specs=[
            block(PROMPT, PROMPT),
            block(PROMPT, HD),
            block(PROMPT, HD),
            whole(PROMPT, HD),
        ],
        out_specs=whole(PROMPT, 2 * HD),
        out_shape=shape((PROMPT, 2 * HD)),
        compiler_params=params(12),
    )(in_hbm(probs), q, g, v)


def response_grad_kernel(lens, probs, q_ref, g_ref, v_ref, part_ref, out_ref, sum_ref, acc):
    i = pl.program_id(0)

    @pl.when(i == 0)
    def _():
        acc[:PROMPT] = part_ref[...]
        acc[PROMPT:] = jnp.zeros((RESP, 2 * HD), f32)

    v1, v2 = v_ref[:PROMPT], v_ref[PROMPT:]
    q = q_ref[...].reshape(AT_ONCE * RESP, HD)
    g = g_ref[...].reshape(AT_ONCE * RESP, HD)
    p1, p2 = probs[0, :PROMPT], probs[0, PROMPT:]
    dp1, dp2 = dot_nt(v1, g), dot_nt(v2, g)
    pb1, pb2 = p1.astype(bf16), p2.astype(bf16)
    delta = jnp.sum(pb1.astype(f32) * dp1, 0, keepdims=True) + jnp.sum(
        pb2.astype(f32) * dp2, 0, keepdims=True
    )
    ds1 = (p1 * (dp1 - delta)).astype(bf16)
    ds2 = (p2 * (dp2 - delta)).astype(bf16)
    acc[:PROMPT, :HD] += dot(ds1, q) * SCALE
    acc[PROMPT:, :HD] += dot(ds2, q) * SCALE
    acc[:PROMPT, HD:] += dot(pb1, g)
    acc[PROMPT:, HD:] += dot(pb2, g)

    @pl.when(i == pl.num_programs(0) - 1)
    def _():
        total = acc[...]
        squares = jnp.sum(total * total, 0, keepdims=True)
        sum_ref[...] = squares[:, :HD] + squares[:, HD:]
        out_ref[:PROMPT] = total[:PROMPT]
        left = total[PROMPT:]
        spread = chosen_rows(lens, 1)
        placed = jnp.zeros((NRESP * RLEN, 2 * HD), f32)
        for _ in range(3):
            term = left.astype(bf16)
            placed = placed + dot(spread, term)
            left = left - term.astype(f32)
        out_ref[PROMPT:] = placed


def response_grad(lens, probs, q, g, v, part):
    n = q.shape[0]
    rows = PROMPT + NRESP * RLEN
    block = lambda *dims: pl.BlockSpec((AT_ONCE,) + dims, lambda i, a: (i, 0, 0))
    whole = lambda *dims: pl.BlockSpec(dims, lambda i, a: (0, 0))
    return pl.pallas_call(
        response_grad_kernel,
        name="response_grad",
        cost_estimate=about(8),
        grid_spec=pltpu.PrefetchScalarGridSpec(
            num_scalar_prefetch=1,
            grid=(n // AT_ONCE,),
            in_specs=[
                pl.BlockSpec((1, LIVE, AT_ONCE * RESP), lambda i, a: (i, 0, 0)),
                block(RESP, HD),
                block(RESP, HD),
                whole(LIVE, HD),
                whole(PROMPT, 2 * HD),
            ],
            out_specs=[whole(rows, 2 * HD), whole(1, HD)],
            scratch_shapes=[pltpu.VMEM((LIVE, 2 * HD), f32)],
        ),
        out_shape=[shape((rows, 2 * HD)), shape((1, HD))],
        compiler_params=params(12),
    )(lens, in_hbm(probs), q, g, v, part)


def ring(step, size=SIDE):
    return [(i, (i + step) % size) for i in range(size)]


def gathered(block, axis):
    return [block] + [lax.ppermute(block, axis, ring(step)) for step in (1, -1, 2)]


def gathered_halves(block, axis):
    low, high = (lax.ppermute(block, axis, ring(step)) for step in (1, -1))
    half = block.shape[0] // 2
    return [
        block,
        low,
        high,
        lax.ppermute(low[:half], axis, ring(1)),
        lax.ppermute(high[half:], axis, ring(-1)),
    ]


def on_device(hidden_stash, key_stash, value_stash, top_grads, lens):
    stage = lax.axis_index("zl")
    my_x = lax.axis_index("x")
    my_y = lax.axis_index("y")
    place = (my_x * SIDE + my_y).reshape(1).astype(jnp.int32)
    qp, qr, gp, gr = pack(lens, place, hidden_stash[0], top_grads)
    parts = jnp.arange(PLANE, dtype=jnp.int32)
    away = lambda slot: jnp.where(slot == 1, 3, jnp.where(slot == 2, 1, jnp.where(slot == 3, 2, 0)))
    outer, inner = away(parts // SIDE), away(parts % SIDE)
    k_from = ((my_x + outer) % SIDE * SIDE + (my_y + inner) % SIDE).astype(jnp.int32)
    v_from = ((my_x + inner) % SIDE * SIDE + (my_y + outer) % SIDE).astype(jnp.int32)
    plane = ("x", "y")
    swap = lambda a: lax.all_to_all(a, plane, 0, 0, tiled=True)
    after = lambda x, y: lax.optimization_barrier((x, y))[0]
    row_k, col_v = stack_live(
        lens, gathered(key_stash[0], "y"), gathered(value_stash[0], "x")
    )
    row_k, col_v, qp = lax.optimization_barrier((row_k, col_v, qp))
    k, v = row_k[0], col_v[0]
    my_qp = swap(qp)
    all_k = gathered_halves(row_k, "x")
    all_v = gathered_halves(col_v, "y")
    my_qr = swap(after(qr, my_qp))
    prob_p, key_p, value_p = prob(True, lens, k_from, v_from, my_qp, all_k, all_v)
    prob_r, key_r, value_r = prob(False, lens, k_from, v_from, my_qr, all_k, all_v)
    stash_p, stash_r = my_qp, my_qr
    busy = (stage >= STAGES // 2).astype(jnp.int32).reshape(1)
    actives = [(stage == now).astype(jnp.int32).reshape(1) for now in range(STAGES)]
    lower = lambda a: lax.ppermute(a, "zl", [(now, now - 1)])
    for now in range(STAGES - 1, -1, -1):
        if now:
            gp, stash_p = chain(True, actives[now], gp, stash_p, prob_p, key_p, value_p)
            if now == STAGES - 2:
                own_p = own_prob(True, 1 - busy, lens, after(qp, gp), k)
                own_r = own_prob(False, 1 - busy, lens, after(qr, own_p), k)
            sent = lower(gp)
            gr = after(gr, gp if now == STAGES - 1 else sent)
            gp = sent
        if now == 1:
            gp, stash_p = chain(True, actives[0], gp, stash_p, prob_p, key_p, value_p)
            own_gp = swap(stash_p)
            gr = after(gr, stash_p)
        gr, stash_r = chain(False, actives[now], gr, stash_r, prob_r, key_r, value_r)
        if now == STAGES - 2:
            gp = after(gp, own_r)
        if now:
            gp = after(gp, gr)
            gr = lower(gr)
    own_p = own_prob(True, busy, lens, after(qp, gr), k, own_p)
    own_gr = swap(stash_r)
    part = prompt_grad(after(own_p, gr), qp, own_gp, v)
    own_r = own_prob(False, busy, lens, after(qr, part), k, own_r)
    raw, squares = response_grad(lens, own_r, qr, own_gr, v, part)
    for axes in (("x", "y", "core"), ("zl", "zh")):
        size = lax.axis_size(axes)
        spread = jnp.broadcast_to(squares, (size, HD))
        squares = jnp.sum(lax.all_to_all(spread, axes, 0, 0, tiled=True), 0, keepdims=True)
    square_sum = jnp.sum(squares)
    entries = STAGES * PLANE * lax.axis_size(("zh", "core")) * raw.shape[0] * raw.shape[1]
    clip_limit = clip_rms * math.sqrt(entries)
    factor = clip_limit / jnp.maximum(jnp.sqrt(square_sum), clip_limit)
    return (raw * factor)[None]


def solution(mesh):
    parts = mesh.devices.reshape(STAGES, SIDE, SIDE, 2, -1)
    finer = Mesh(parts, ("zl", "x", "y", "zh", "core"))
    tp = ("zh", "core")
    pipe = ("zl", "x", "y")
    placed = (
        P(pipe, None, tp),
        P(pipe, None, tp),
        P(pipe, None, tp),
        P(None, tp),
        P(),
    )
    return jax.shard_map(
        on_device, mesh=finer, in_specs=placed, out_specs=P(pipe, None, tp), check_vma=False
    )
```

```python
import functools
import math

import jax
import jax.numpy as jnp
from jax import lax
from jax.experimental import pallas as pl
from jax.experimental.pallas import tpu as pltpu
from jax.sharding import Mesh, PartitionSpec as P

HD = 128
PROMPT = 256
NRESP = 4
RLEN = 64
RESP = 192
LIVE = PROMPT + RESP
STAGES = 4
SIDE = 4
PLANE = SIDE * SIDE

clip_rms = 0.5
SCALE = 1.0 / math.sqrt(HD)
EXP2_SCALE = SCALE * math.log2(math.e)
f32 = jnp.float32
bf16 = jnp.bfloat16


VMEM = pl.BlockSpec(memory_space=pltpu.VMEM)
SMEM = pl.BlockSpec(memory_space=pltpu.SMEM)
HBM = pl.BlockSpec(memory_space=pltpu.HBM)


def dot(a, b):
    return lax.dot_general(a, b, (((1,), (0,)), ((), ())), preferred_element_type=f32)


def dot_nt(a, b):
    return lax.dot_general(a, b, (((1,), (1,)), ((), ())), preferred_element_type=f32)


def about(us):
    return pl.CostEstimate(flops=us * 1_000_000_000, bytes_accessed=0, transcendentals=0)


def params(mebibytes=24):
    return pltpu.CompilerParams(vmem_limit_bytes=mebibytes << 20)


def shape(dims, dtype=f32):
    return jax.ShapeDtypeStruct(dims, dtype)


def starts(lens):
    first = lens[0]
    second = first + lens[1]
    return first, second, second + lens[2]


def start_of(row, lens):
    one, two, three = starts(lens)
    return jnp.where(
        row >= three, three, jnp.where(row >= two, two, jnp.where(row >= one, one, 0))
    )


def prompt_bias(query_dim):
    q = lax.broadcasted_iota(jnp.int32, (PROMPT, PROMPT), query_dim)
    k = lax.broadcasted_iota(jnp.int32, (PROMPT, PROMPT), 1 - query_dim)
    return jnp.where(k <= q, 0.0, -jnp.inf).astype(f32)


def response_bias(lens, query_dim, repeats=1):
    dims = (RESP, repeats * RESP)
    q = lax.broadcasted_iota(jnp.int32, dims, query_dim)
    k = lax.broadcasted_iota(jnp.int32, dims, 1 - query_dim)
    for _ in range(repeats - 1):
        q = jnp.where(q >= RESP, q - RESP, q)
    return jnp.where((k <= q) & (k >= start_of(q, lens)), 0.0, -jnp.inf).astype(f32)


def chosen_rows(lens, row_dim):
    dims = (RESP, NRESP * RLEN) if row_dim == 0 else (NRESP * RLEN, RESP)
    row = lax.broadcasted_iota(jnp.int32, dims, row_dim)
    col = lax.broadcasted_iota(jnp.int32, dims, 1 - row_dim)
    one, two, three = starts(lens)
    slot = (
        (row >= one).astype(jnp.int32)
        + (row >= two).astype(jnp.int32)
        + (row >= three).astype(jnp.int32)
    )
    return jnp.where(col == slot * RLEN + row - start_of(row, lens), 1.0, 0.0).astype(bf16)


def pack_kernel(lens, place, x_ref, top_ref, xp_out, xr_out, tp_out, tr_out, chosen):
    @pl.when(pl.program_id(0) == 0)
    def _():
        pick = chosen_rows(lens, 0)
        chosen[...] = pick
        tp_out[...] = top_ref[:PROMPT]
        tr_out[...] = dot(pick, top_ref[PROMPT:]).astype(bf16)

    live = dot(chosen[...], x_ref[PROMPT:]).astype(bf16)
    for h in range(x_ref.shape[1] // HD):
        cols = slice(h * HD, (h + 1) * HD)
        xp_out[h] = x_ref[:PROMPT, cols]
        xr_out[h] = live[:, cols]


def pack(lens, place, x, top):
    rows, width = x.shape
    heads = width // HD
    steps = 2
    some = heads // steps
    whole = lambda n: pl.BlockSpec((n, HD), lambda i, l, p: (0, 0))
    return pl.pallas_call(
        pack_kernel,
        name="pack",
        cost_estimate=about(4),
        grid_spec=pltpu.PrefetchScalarGridSpec(
            num_scalar_prefetch=2,
            grid=(steps,),
            in_specs=[
                pl.BlockSpec((rows, some * HD), lambda i, l, p: (0, i)),
                pl.BlockSpec((rows, HD), lambda i, l, p: (0, p[0])),
            ],
            out_specs=[
                pl.BlockSpec((some, PROMPT, HD), lambda i, l, p: (i, 0, 0)),
                pl.BlockSpec((some, RESP, HD), lambda i, l, p: (i, 0, 0)),
                whole(PROMPT),
                whole(RESP),
            ],
            scratch_shapes=[pltpu.VMEM((RESP, NRESP * RLEN), bf16)],
        ),
        out_shape=[
            shape((heads, PROMPT, HD), bf16),
            shape((heads, RESP, HD), bf16),
            shape((PROMPT, HD), bf16),
            shape((RESP, HD), bf16),
        ],
        compiler_params=params(60),
    )(lens, place, x, top)


def stack_live_kernel(lens, *refs):
    out_k, out_v = refs[2 * SIDE :]
    chosen = chosen_rows(lens, 0)
    for parts, out in ((refs[:SIDE], out_k), (refs[SIDE : 2 * SIDE], out_v)):
        for i, part in enumerate(parts):
            out[i, :PROMPT] = part[:PROMPT]
            out[i, PROMPT:] = dot(chosen, part[PROMPT:]).astype(bf16)


def stack_live(lens, keys, values):
    return pl.pallas_call(
        stack_live_kernel,
        name="stack_live",
        cost_estimate=about(2),
        in_specs=[SMEM] + [VMEM] * (2 * SIDE),
        out_specs=[VMEM] * 2,
        out_shape=[shape((SIDE, LIVE, HD), bf16)] * 2,
        compiler_params=params(8),
    )(lens, *keys, *values)


def softmax(scores, dim):
    top = functools.reduce(jnp.maximum, [jnp.max(x, dim, keepdims=True) for x in scores])
    weights = [jnp.exp2((x - top) * EXP2_SCALE) for x in scores]
    total = functools.reduce(jnp.add, [jnp.sum(w, dim, keepdims=True) for w in weights])
    share = 1.0 / total
    return [w * share for w in weights]


AT_ONCE = 4
PROMPT_ROW = PROMPT + HD
RESP_ROW = 2 * PROMPT + HD
def in_hbm(x):
    return pltpu.with_memory_space_constraint(x, pltpu.HBM)


def prob_kernel(prompt, lens, k_from, v_from, q_ref, *refs):
    half = (len(refs) - 9) // 2
    k_parts, v_parts = refs[:half], refs[half : 2 * half]
    probs_out, keys_out, values_out, probs, keys, values, bias, sems, kv_sems = refs[2 * half :]
    n, count, _ = keys.shape
    bias[...] = prompt_bias(0) if prompt else response_bias(lens, 0)
    for parts, held, table in ((k_parts, keys, k_from), (v_parts, values, v_from)):
        at = 0
        for part in parts:
            for i in range(part.shape[0]):
                held[table[at]] = part[i, :count]
                at += 1
    ordered = [
        pltpu.make_async_copy(held, out, kv_sems.at[j])
        for j, (held, out) in enumerate(((keys, keys_out), (values, values_out)))
    ]
    for copy in ordered:
        copy.start()

    def done(i):
        some = pl.ds(i * AT_ONCE, AT_ONCE)
        return pltpu.make_async_copy(probs.at[some], probs_out.at[some], sems.at[i])

    def body(i, carry):
        for u in range(AT_ONCE):
            layer = i * AT_ONCE + u
            q, k, v = q_ref[layer], keys[layer], values[layer]
            if prompt:
                (p,) = softmax([dot_nt(q, k) + bias[...]], -1)
                probs[layer, :, :PROMPT] = p
                probs[layer, :, PROMPT:] = dot(p.astype(bf16), v)
            else:
                p1, p2 = softmax([dot_nt(q, k[:PROMPT]), dot_nt(q, k[PROMPT:]) + bias[...]], -1)
                probs[layer, :, :PROMPT] = p1
                probs[layer, :, PROMPT:LIVE] = p2
                probs[layer, :, 2 * PROMPT :] = dot(p1.astype(bf16), v[:PROMPT]) + dot(
                    p2.astype(bf16), v[PROMPT:]
                )
        done(i).start()
        return carry

    lax.fori_loop(0, n // AT_ONCE, body, 0)
    for copy in ordered + [done(i) for i in range(n // AT_ONCE)]:
        copy.wait()


def prob(prompt, lens, k_from, v_from, q, k, v):
    n, rows, _ = q.shape
    count, width = (PROMPT, PROMPT_ROW) if prompt else (LIVE, RESP_ROW)
    results = [((n, rows, width), f32), ((n, count, HD), bf16), ((n, count, HD), bf16)]
    return pl.pallas_call(
        functools.partial(prob_kernel, prompt),
        name="prompt_prob" if prompt else "response_prob",
        cost_estimate=about(7),
        in_specs=[SMEM] * 3 + [VMEM] * (1 + len(k) + len(v)),
        out_specs=[HBM] * 3,
        scratch_shapes=[pltpu.VMEM(*r) for r in results]
        + [
            pltpu.VMEM((rows, rows), f32),
            pltpu.SemaphoreType.DMA((n // AT_ONCE,)),
            pltpu.SemaphoreType.DMA((2,)),
        ],
        out_shape=[pltpu.HBM(*r) for r in results],
        compiler_params=params(22),
    )(lens, k_from, v_from, q, *k, *v)


GROUPS = ((15, 16), (14, 15), (12, 14), (10, 12), (8, 10), (6, 8), (4, 6), (2, 4), (0, 2))
AHEAD = 4
SAVES = 4


def chain_kernel(prompt, active, g_in, stash_in, probs_in, keys_in, values_in, g_out, stash, probs, keys, values, grads, sems, save_sems):
    n = keys.shape[0]

    def loads(j):
        span = pl.ds(GROUPS[j][0], GROUPS[j][1] - GROUPS[j][0])
        return [
            pltpu.make_async_copy(source.at[span], held.at[span], sems.at[j, i])
            for i, (source, held) in enumerate(
                ((values_in, values), (probs_in, probs), (keys_in, keys))
            )
        ]

    def step(layer):
        d = grads[layer]
        wide = d.astype(f32)
        k, v = keys[layer], values[layer]
        if prompt:
            delta = jnp.sum(wide * probs[layer, :, PROMPT:], -1, keepdims=True)
            ds = (probs[layer, :, :PROMPT] * (dot_nt(d, v) - delta)).astype(bf16)
            change = dot(ds, k)
        else:
            delta = jnp.sum(wide * probs[layer, :, 2 * PROMPT :], -1, keepdims=True)
            ds1 = (probs[layer, :, :PROMPT] * (dot_nt(d, v[:PROMPT]) - delta)).astype(bf16)
            ds2 = (probs[layer, :, PROMPT:LIVE] * (dot_nt(d, v[PROMPT:]) - delta)).astype(bf16)
            change = dot(ds1, k[:PROMPT]) + dot(ds2, k[PROMPT:])
        return (wide + change * SCALE).astype(bf16)

    def save(j):
        some = pl.ds(j * (n // SAVES), n // SAVES)
        return pltpu.make_async_copy(grads.at[some], stash.at[some], save_sems.at[j])

    @pl.when(active[0] == 1)
    def _():
        for j in range(AHEAD):
            for copy in loads(j):
                copy.start()
        grads[n - 1] = g_in[...]
        for j, (low, high) in enumerate(GROUPS):
            for copy in loads(j):
                copy.wait()
            if j + AHEAD < len(GROUPS):
                for copy in loads(j + AHEAD):
                    copy.start()

            def body(i, carry, high=high):
                grads[high - 2 - i] = step(high - 1 - i)
                return carry

            if high - low == 1:
                body(0, 0)
            else:
                lax.fori_loop(0, high - max(low, 1), body, 0)
            if low and low % (n // SAVES) == 0:
                save(low // (n // SAVES)).start()
        save(0).start()
        g_out[...] = step(0)
        for j in range(SAVES):
            save(j).wait()


def chain(prompt, active, g, stash, probs, k, v):
    n, rows, _ = probs.shape
    anywhere = pl.BlockSpec(memory_space=pl.ANY)
    return pl.pallas_call(
        functools.partial(chain_kernel, prompt),
        name="prompt_chain" if prompt else "response_chain",
        cost_estimate=about(7),
        in_specs=[SMEM, VMEM, anywhere] + [HBM] * 3,
        out_specs=[VMEM, anywhere],
        scratch_shapes=[
            pltpu.VMEM(probs.shape, f32),
            pltpu.VMEM(k.shape, bf16),
            pltpu.VMEM(v.shape, bf16),
            pltpu.VMEM((n, rows, HD), bf16),
            pltpu.SemaphoreType.DMA((len(GROUPS), 3)),
            pltpu.SemaphoreType.DMA((SAVES,)),
        ],
        out_shape=[shape((rows, HD), bf16), shape((n, rows, HD), bf16)],
        input_output_aliases={2: 1},
        compiler_params=params(22),
    )(active, g, stash, in_hbm(probs), in_hbm(k), in_hbm(v))


HEADS_AT_ONCE = 2


def own_prob_kernel(prompt, active, lens, q_ref, k_ref, *refs):
    out, probs, queries, bias, sems, q_sem = refs[-6:]
    steps = queries.shape[0] // AT_ONCE

    def done(i):
        some = pl.ds(i * AT_ONCE, AT_ONCE) if prompt else pl.ds(i, 1)
        return pltpu.make_async_copy(probs.at[some], out.at[some], sems.at[i])

    @pl.when(active[0] == 1)
    def _():
        fetch = pltpu.make_async_copy(q_ref, queries, q_sem)
        fetch.start()
        if prompt:
            bias[...] = prompt_bias(1)
        else:
            bias[...] = response_bias(lens, 1, AT_ONCE)
        k1, k2 = k_ref[:PROMPT], k_ref[PROMPT:]
        fetch.wait()

        def body(i, carry):
            if prompt:
                for u in range(AT_ONCE):
                    head = i * AT_ONCE + u
                    (probs[head],) = softmax([dot_nt(k1, queries[head]) + bias[...]], 0)
            else:
                q = queries[pl.ds(i * AT_ONCE, AT_ONCE)].reshape(AT_ONCE * RESP, HD)
                p1, p2 = softmax([dot_nt(k1, q), dot_nt(k2, q) + bias[...]], 0)
                probs[i, :PROMPT] = p1
                probs[i, PROMPT:] = p2
            done(i).start()
            return carry

        lax.fori_loop(0, steps, body, 0)
        for i in range(steps):
            done(i).wait()


def own_prob(prompt, active, lens, q, k, earlier=None, us=5):
    n, rows, _ = q.shape
    dims = (n, PROMPT, rows) if prompt else (n // AT_ONCE, LIVE, AT_ONCE * RESP)
    more = [] if earlier is None else [in_hbm(earlier)]
    return pl.pallas_call(
        functools.partial(own_prob_kernel, prompt),
        name="own_prompt_prob" if prompt else "own_response_prob",
        cost_estimate=about(us),
        in_specs=[SMEM, SMEM, HBM, VMEM] + [HBM] * len(more),
        out_specs=HBM,
        scratch_shapes=[
            pltpu.VMEM(dims, f32),
            pltpu.VMEM(q.shape, bf16),
            pltpu.VMEM((rows, rows if prompt else AT_ONCE * RESP), f32),
            pltpu.SemaphoreType.DMA((n // AT_ONCE,)),
            pltpu.SemaphoreType.DMA,
        ],
        out_shape=pltpu.HBM(dims, f32),
        input_output_aliases={4: 0} if more else {},
        compiler_params=params(16),
    )(active, lens, in_hbm(q), k, *more)


def prompt_grad_kernel(probs, q_ref, g_ref, v_ref, out_ref):
    @pl.when(pl.program_id(0) == 0)
    def _():
        out_ref[...] = jnp.zeros_like(out_ref)

    v = v_ref[...]

    def body(j, carry):
        dk, dv = 0.0, 0.0
        for i in range(HEADS_AT_ONCE):
            u = j * HEADS_AT_ONCE + i
            q, g, p = q_ref[u], g_ref[u], probs[u]
            dp = dot_nt(v, g)
            pb = p.astype(bf16)
            delta = jnp.sum(pb.astype(f32) * dp, 0, keepdims=True)
            ds = (p * (dp - delta)).astype(bf16)
            dk = dk + dot(ds, q)
            dv = dv + dot(pb, g)
        out_ref[:, :HD] += dk * SCALE
        out_ref[:, HD:] += dv
        return carry

    lax.fori_loop(0, q_ref.shape[0] // HEADS_AT_ONCE, body, 0)


def prompt_grad(probs, q, g, v):
    n = q.shape[0]
    block = lambda *dims: pl.BlockSpec((AT_ONCE,) + dims, lambda i: (i, 0, 0))
    whole = lambda *dims: pl.BlockSpec(dims, lambda i: (0, 0))
    return pl.pallas_call(
        prompt_grad_kernel,
        name="prompt_grad",
        cost_estimate=about(5),
        grid=(n // AT_ONCE,),
        in_specs=[
            block(PROMPT, PROMPT),
            block(PROMPT, HD),
            block(PROMPT, HD),
            whole(PROMPT, HD),
        ],
        out_specs=whole(PROMPT, 2 * HD),
        out_shape=shape((PROMPT, 2 * HD)),
        compiler_params=params(12),
    )(in_hbm(probs), q, g, v)


def response_grad_kernel(lens, probs, q_ref, g_ref, v_ref, part_ref, out_ref, sum_ref, acc):
    i = pl.program_id(0)

    @pl.when(i == 0)
    def _():
        acc[:PROMPT] = part_ref[...]
        acc[PROMPT:] = jnp.zeros((RESP, 2 * HD), f32)

    v1, v2 = v_ref[:PROMPT], v_ref[PROMPT:]
    q = q_ref[...].reshape(AT_ONCE * RESP, HD)
    g = g_ref[...].reshape(AT_ONCE * RESP, HD)
    p1, p2 = probs[0, :PROMPT], probs[0, PROMPT:]
    dp1, dp2 = dot_nt(v1, g), dot_nt(v2, g)
    pb1, pb2 = p1.astype(bf16), p2.astype(bf16)
    delta = jnp.sum(pb1.astype(f32) * dp1, 0, keepdims=True) + jnp.sum(
        pb2.astype(f32) * dp2, 0, keepdims=True
    )
    ds1 = (p1 * (dp1 - delta)).astype(bf16)
    ds2 = (p2 * (dp2 - delta)).astype(bf16)
    acc[:PROMPT, :HD] += dot(ds1, q) * SCALE
    acc[PROMPT:, :HD] += dot(ds2, q) * SCALE
    acc[:PROMPT, HD:] += dot(pb1, g)
    acc[PROMPT:, HD:] += dot(pb2, g)

    @pl.when(i == pl.num_programs(0) - 1)
    def _():
        total = acc[...]
        squares = jnp.sum(total * total, 0, keepdims=True)
        sum_ref[...] = squares[:, :HD] + squares[:, HD:]
        out_ref[:PROMPT] = total[:PROMPT]
        left = total[PROMPT:]
        spread = chosen_rows(lens, 1)
        placed = jnp.zeros((NRESP * RLEN, 2 * HD), f32)
        for _ in range(3):
            term = left.astype(bf16)
            placed = placed + dot(spread, term)
            left = left - term.astype(f32)
        out_ref[PROMPT:] = placed


def response_grad(lens, probs, q, g, v, part):
    n = q.shape[0]
    rows = PROMPT + NRESP * RLEN
    block = lambda *dims: pl.BlockSpec((AT_ONCE,) + dims, lambda i, a: (i, 0, 0))
    whole = lambda *dims: pl.BlockSpec(dims, lambda i, a: (0, 0))
    return pl.pallas_call(
        response_grad_kernel,
        name="response_grad",
        cost_estimate=about(8),
        grid_spec=pltpu.PrefetchScalarGridSpec(
            num_scalar_prefetch=1,
            grid=(n // AT_ONCE,),
            in_specs=[
                pl.BlockSpec((1, LIVE, AT_ONCE * RESP), lambda i, a: (i, 0, 0)),
                block(RESP, HD),
                block(RESP, HD),
                whole(LIVE, HD),
                whole(PROMPT, 2 * HD),
            ],
            out_specs=[whole(rows, 2 * HD), whole(1, HD)],
            scratch_shapes=[pltpu.VMEM((LIVE, 2 * HD), f32)],
        ),
        out_shape=[shape((rows, 2 * HD)), shape((1, HD))],
        compiler_params=params(12),
    )(lens, in_hbm(probs), q, g, v, part)


def ring(step, size=SIDE):
    return [(i, (i + step) % size) for i in range(size)]


def gathered(block, axis):
    return [block] + [lax.ppermute(block, axis, ring(step)) for step in (1, -1, 2)]


def gathered_halves(block, axis):
    low, high = (lax.ppermute(block, axis, ring(step)) for step in (1, -1))
    half = block.shape[0] // 2
    return [
        block,
        low,
        high,
        lax.ppermute(low[:half], axis, ring(1)),
        lax.ppermute(high[half:], axis, ring(-1)),
    ]


def on_device(hidden_stash, key_stash, value_stash, top_grads, lens):
    stage = lax.axis_index("zl")
    my_x = lax.axis_index("x")
    my_y = lax.axis_index("y")
    place = (my_x * SIDE + my_y).reshape(1).astype(jnp.int32)
    qp, qr, gp, gr = pack(lens, place, hidden_stash[0], top_grads)
    parts = jnp.arange(PLANE, dtype=jnp.int32)
    away = lambda slot: jnp.where(slot == 1, 3, jnp.where(slot == 2, 1, jnp.where(slot == 3, 2, 0)))
    outer, inner = away(parts // SIDE), away(parts % SIDE)
    k_from = ((my_x + outer) % SIDE * SIDE + (my_y + inner) % SIDE).astype(jnp.int32)
    v_from = ((my_x + inner) % SIDE * SIDE + (my_y + outer) % SIDE).astype(jnp.int32)
    plane = ("x", "y")
    swap = lambda a: lax.all_to_all(a, plane, 0, 0, tiled=True)
    after = lambda x, y: lax.optimization_barrier((x, y))[0]
    row_k, col_v = stack_live(
        lens, gathered(key_stash[0], "y"), gathered(value_stash[0], "x")
    )
    row_k, col_v, qp = lax.optimization_barrier((row_k, col_v, qp))
    k, v = row_k[0], col_v[0]
    my_qp = swap(qp)
    all_k = gathered_halves(row_k, "x")
    all_v = gathered_halves(col_v, "y")
    my_qr = swap(after(qr, my_qp))
    prob_p, key_p, value_p = prob(True, lens, k_from, v_from, my_qp, all_k, all_v)
    prob_r, key_r, value_r = prob(False, lens, k_from, v_from, my_qr, all_k, all_v)
    stash_p, stash_r = my_qp, my_qr
    busy = (stage >= STAGES // 2).astype(jnp.int32).reshape(1)
    actives = [(stage == now).astype(jnp.int32).reshape(1) for now in range(STAGES)]
    lower = lambda a: lax.ppermute(a, "zl", [(now, now - 1)])
    for now in range(STAGES - 1, -1, -1):
        if now:
            gp, stash_p = chain(True, actives[now], gp, stash_p, prob_p, key_p, value_p)
            if now == STAGES - 2:
                own_p = own_prob(True, 1 - busy, lens, after(qp, gp), k)
                own_r = own_prob(False, 1 - busy, lens, after(qr, own_p), k)
            sent = lower(gp)
            gr = after(gr, gp if now == STAGES - 1 else sent)
            gp = sent
        if now == 1:
            gp, stash_p = chain(True, actives[0], gp, stash_p, prob_p, key_p, value_p)
            own_gp = swap(stash_p)
            gr = after(gr, stash_p)
        gr, stash_r = chain(False, actives[now], gr, stash_r, prob_r, key_r, value_r)
        if now == STAGES - 2:
            gp = after(gp, own_r)
        if now:
            gp = after(gp, gr)
            gr = lower(gr)
    own_p = own_prob(True, busy, lens, after(qp, gr), k, own_p)
    own_gr = swap(stash_r)
    part = prompt_grad(after(own_p, gr), qp, own_gp, v)
    own_r = own_prob(False, busy, lens, after(qr, part), k, own_r)
    raw, squares = response_grad(lens, own_r, qr, own_gr, v, part)
    for axes in (("x", "y", "core"), ("zl", "zh")):
        size = lax.axis_size(axes)
        spread = jnp.broadcast_to(squares, (size, HD))
        squares = jnp.sum(lax.all_to_all(spread, axes, 0, 0, tiled=True), 0, keepdims=True)
    square_sum = jnp.sum(squares)
    entries = STAGES * PLANE * lax.axis_size(("zh", "core")) * raw.shape[0] * raw.shape[1]
    clip_limit = clip_rms * math.sqrt(entries)
    factor = clip_limit / jnp.maximum(jnp.sqrt(square_sum), clip_limit)
    return (raw * factor)[None]


def solution(mesh):
    parts = mesh.devices.reshape(STAGES, SIDE, SIDE, 2, -1)
    finer = Mesh(parts, ("zl", "x", "y", "zh", "core"))
    tp = ("zh", "core")
    pipe = ("zl", "x", "y")
    placed = (
        P(pipe, None, tp),
        P(pipe, None, tp),
        P(pipe, None, tp),
        P(None, tp),
        P(),
    )
    return jax.shard_map(
        on_device, mesh=finer, in_specs=placed, out_specs=P(pipe, None, tp), check_vma=False
    )
```

```python
import functools
import math

import jax
import jax.numpy as jnp
from jax import lax
from jax.experimental import pallas as pl
from jax.experimental.pallas import tpu as pltpu
from jax.sharding import Mesh, PartitionSpec as P

HD = 128
PROMPT = 256
NRESP = 4
RLEN = 64
RESP = 192
LIVE = PROMPT + RESP
STAGES = 4
SIDE = 4
PLANE = SIDE * SIDE

clip_rms = 0.5
SCALE = 1.0 / math.sqrt(HD)
EXP2_SCALE = SCALE * math.log2(math.e)
f32 = jnp.float32
bf16 = jnp.bfloat16


VMEM = pl.BlockSpec(memory_space=pltpu.VMEM)
SMEM = pl.BlockSpec(memory_space=pltpu.SMEM)
HBM = pl.BlockSpec(memory_space=pltpu.HBM)


def dot(a, b):
    return lax.dot_general(a, b, (((1,), (0,)), ((), ())), preferred_element_type=f32)


def dot_nt(a, b):
    return lax.dot_general(a, b, (((1,), (1,)), ((), ())), preferred_element_type=f32)


def about(us):
    return pl.CostEstimate(flops=us * 1_000_000_000, bytes_accessed=0, transcendentals=0)


def params(mebibytes=24):
    return pltpu.CompilerParams(vmem_limit_bytes=mebibytes << 20)


def shape(dims, dtype=f32):
    return jax.ShapeDtypeStruct(dims, dtype)


def starts(lens):
    first = lens[0]
    second = first + lens[1]
    return first, second, second + lens[2]


def start_of(row, lens):
    one, two, three = starts(lens)
    return jnp.where(
        row >= three, three, jnp.where(row >= two, two, jnp.where(row >= one, one, 0))
    )


def prompt_bias(query_dim):
    q = lax.broadcasted_iota(jnp.int32, (PROMPT, PROMPT), query_dim)
    k = lax.broadcasted_iota(jnp.int32, (PROMPT, PROMPT), 1 - query_dim)
    return jnp.where(k <= q, 0.0, -jnp.inf).astype(f32)


def response_bias(lens, query_dim, repeats=1):
    dims = (RESP, repeats * RESP)
    q = lax.broadcasted_iota(jnp.int32, dims, query_dim)
    k = lax.broadcasted_iota(jnp.int32, dims, 1 - query_dim)
    for _ in range(repeats - 1):
        q = jnp.where(q >= RESP, q - RESP, q)
    return jnp.where((k <= q) & (k >= start_of(q, lens)), 0.0, -jnp.inf).astype(f32)


def chosen_rows(lens, row_dim):
    dims = (RESP, NRESP * RLEN) if row_dim == 0 else (NRESP * RLEN, RESP)
    row = lax.broadcasted_iota(jnp.int32, dims, row_dim)
    col = lax.broadcasted_iota(jnp.int32, dims, 1 - row_dim)
    one, two, three = starts(lens)
    slot = (
        (row >= one).astype(jnp.int32)
        + (row >= two).astype(jnp.int32)
        + (row >= three).astype(jnp.int32)
    )
    return jnp.where(col == slot * RLEN + row - start_of(row, lens), 1.0, 0.0).astype(bf16)


def pack_kernel(lens, place, x_ref, top_ref, xp_out, xr_out, tp_out, tr_out, chosen):
    @pl.when(pl.program_id(0) == 0)
    def _():
        pick = chosen_rows(lens, 0)
        chosen[...] = pick
        tp_out[...] = top_ref[:PROMPT]
        tr_out[...] = dot(pick, top_ref[PROMPT:]).astype(bf16)

    live = dot(chosen[...], x_ref[PROMPT:]).astype(bf16)
    for h in range(x_ref.shape[1] // HD):
        cols = slice(h * HD, (h + 1) * HD)
        xp_out[h] = x_ref[:PROMPT, cols]
        xr_out[h] = live[:, cols]


def pack(lens, place, x, top):
    rows, width = x.shape
    heads = width // HD
    steps = 2
    some = heads // steps
    whole = lambda n: pl.BlockSpec((n, HD), lambda i, l, p: (0, 0))
    return pl.pallas_call(
        pack_kernel,
        name="pack",
        cost_estimate=about(4),
        grid_spec=pltpu.PrefetchScalarGridSpec(
            num_scalar_prefetch=2,
            grid=(steps,),
            in_specs=[
                pl.BlockSpec((rows, some * HD), lambda i, l, p: (0, i)),
                pl.BlockSpec((rows, HD), lambda i, l, p: (0, p[0])),
            ],
            out_specs=[
                pl.BlockSpec((some, PROMPT, HD), lambda i, l, p: (i, 0, 0)),
                pl.BlockSpec((some, RESP, HD), lambda i, l, p: (i, 0, 0)),
                whole(PROMPT),
                whole(RESP),
            ],
            scratch_shapes=[pltpu.VMEM((RESP, NRESP * RLEN), bf16)],
        ),
        out_shape=[
            shape((heads, PROMPT, HD), bf16),
            shape((heads, RESP, HD), bf16),
            shape((PROMPT, HD), bf16),
            shape((RESP, HD), bf16),
        ],
        compiler_params=params(60),
    )(lens, place, x, top)


def stack_live_kernel(lens, *refs):
    out_k, out_v = refs[2 * SIDE :]
    chosen = chosen_rows(lens, 0)
    for parts, out in ((refs[:SIDE], out_k), (refs[SIDE : 2 * SIDE], out_v)):
        for i, part in enumerate(parts):
            out[i, :PROMPT] = part[:PROMPT]
            out[i, PROMPT:] = dot(chosen, part[PROMPT:]).astype(bf16)


def stack_live(lens, keys, values):
    return pl.pallas_call(
        stack_live_kernel,
        name="stack_live",
        cost_estimate=about(2),
        in_specs=[SMEM] + [VMEM] * (2 * SIDE),
        out_specs=[VMEM] * 2,
        out_shape=[shape((SIDE, LIVE, HD), bf16)] * 2,
        compiler_params=params(8),
    )(lens, *keys, *values)


def softmax(scores, dim):
    top = functools.reduce(jnp.maximum, [jnp.max(x, dim, keepdims=True) for x in scores])
    weights = [jnp.exp2((x - top) * EXP2_SCALE) for x in scores]
    total = functools.reduce(jnp.add, [jnp.sum(w, dim, keepdims=True) for w in weights])
    share = 1.0 / total
    return [w * share for w in weights]


AT_ONCE = 4
SENT = 2
PROMPT_ROW = PROMPT + HD
RESP_ROW = 2 * PROMPT + HD
def in_hbm(x):
    return pltpu.with_memory_space_constraint(x, pltpu.HBM)


def prob_kernel(prompt, lens, k_from, v_from, q_ref, *refs):
    half = (len(refs) - 9) // 2
    k_parts, v_parts = refs[:half], refs[half : 2 * half]
    probs_out, keys_out, values_out, probs, keys, values, bias, sems, kv_sems = refs[2 * half :]
    n, count, _ = keys.shape
    bias[...] = prompt_bias(0) if prompt else response_bias(lens, 0)
    for parts, held, table in ((k_parts, keys, k_from), (v_parts, values, v_from)):
        at = 0
        for part in parts:
            for i in range(part.shape[0]):
                held[table[at]] = part[i, :count]
                at += 1
    ordered = [
        pltpu.make_async_copy(held, out, kv_sems.at[j])
        for j, (held, out) in enumerate(((keys, keys_out), (values, values_out)))
    ]
    for copy in ordered:
        copy.start()

    def done(i):
        some = pl.ds(i * SENT, SENT)
        return pltpu.make_async_copy(probs.at[some], probs_out.at[some], sems.at[i])

    def body(i, carry):
        for u in range(AT_ONCE):
            layer = i * AT_ONCE + u
            q, k, v = q_ref[layer], keys[layer], values[layer]
            if prompt:
                (p,) = softmax([dot_nt(q, k) + bias[...]], -1)
                probs[layer, :, :PROMPT] = p
                probs[layer, :, PROMPT:] = dot(p.astype(bf16), v)
            else:
                p1, p2 = softmax([dot_nt(q, k[:PROMPT]), dot_nt(q, k[PROMPT:]) + bias[...]], -1)
                probs[layer, :, :PROMPT] = p1
                probs[layer, :, PROMPT:LIVE] = p2
                probs[layer, :, 2 * PROMPT :] = dot(p1.astype(bf16), v[:PROMPT]) + dot(
                    p2.astype(bf16), v[PROMPT:]
                )
            if u % SENT == SENT - 1:
                done(i * (AT_ONCE // SENT) + u // SENT).start()
        return carry

    lax.fori_loop(0, n // AT_ONCE, body, 0)
    for copy in ordered + [done(i) for i in range(n // SENT)]:
        copy.wait()


def prob(prompt, lens, k_from, v_from, q, k, v):
    n, rows, _ = q.shape
    count, width = (PROMPT, PROMPT_ROW) if prompt else (LIVE, RESP_ROW)
    results = [((n, rows, width), f32), ((n, count, HD), bf16), ((n, count, HD), bf16)]
    return pl.pallas_call(
        functools.partial(prob_kernel, prompt),
        name="prompt_prob" if prompt else "response_prob",
        cost_estimate=about(7),
        in_specs=[SMEM] * 3 + [VMEM] * (1 + len(k) + len(v)),
        out_specs=[HBM] * 3,
        scratch_shapes=[pltpu.VMEM(*r) for r in results]
        + [
            pltpu.VMEM((rows, rows), f32),
            pltpu.SemaphoreType.DMA((n // SENT,)),
            pltpu.SemaphoreType.DMA((2,)),
        ],
        out_shape=[pltpu.HBM(*r) for r in results],
        compiler_params=params(22),
    )(lens, k_from, v_from, q, *k, *v)


GROUPS = ((15, 16), (14, 15), (12, 14), (10, 12), (8, 10), (6, 8), (4, 6), (2, 4), (0, 2))
AHEAD = 4
SAVES = 4


def chain_kernel(prompt, active, g_in, stash_in, probs_in, keys_in, values_in, g_out, stash, probs, keys, values, grads, sems, save_sems):
    n = keys.shape[0]

    def loads(j):
        span = pl.ds(GROUPS[j][0], GROUPS[j][1] - GROUPS[j][0])
        return [
            pltpu.make_async_copy(source.at[span], held.at[span], sems.at[j, i])
            for i, (source, held) in enumerate(
                ((values_in, values), (probs_in, probs), (keys_in, keys))
            )
        ]

    def step(layer):
        d = grads[layer]
        wide = d.astype(f32)
        k, v = keys[layer], values[layer]
        if prompt:
            delta = jnp.sum(wide * probs[layer, :, PROMPT:], -1, keepdims=True)
            ds = (probs[layer, :, :PROMPT] * (dot_nt(d, v) - delta)).astype(bf16)
            change = dot(ds, k)
        else:
            delta = jnp.sum(wide * probs[layer, :, 2 * PROMPT :], -1, keepdims=True)
            ds1 = (probs[layer, :, :PROMPT] * (dot_nt(d, v[:PROMPT]) - delta)).astype(bf16)
            ds2 = (probs[layer, :, PROMPT:LIVE] * (dot_nt(d, v[PROMPT:]) - delta)).astype(bf16)
            change = dot(ds1, k[:PROMPT]) + dot(ds2, k[PROMPT:])
        return (wide + change * SCALE).astype(bf16)

    def save(j):
        some = pl.ds(j * (n // SAVES), n // SAVES)
        return pltpu.make_async_copy(grads.at[some], stash.at[some], save_sems.at[j])

    @pl.when(active[0] == 1)
    def _():
        for j in range(AHEAD):
            for copy in loads(j):
                copy.start()
        grads[n - 1] = g_in[...]
        for j, (low, high) in enumerate(GROUPS):
            for copy in loads(j):
                copy.wait()
            if j + AHEAD < len(GROUPS):
                for copy in loads(j + AHEAD):
                    copy.start()

            def body(i, carry, high=high):
                grads[high - 2 - i] = step(high - 1 - i)
                return carry

            if high - low == 1:
                body(0, 0)
            else:
                lax.fori_loop(0, high - max(low, 1), body, 0)
            if low and low % (n // SAVES) == 0:
                save(low // (n // SAVES)).start()
        save(0).start()
        g_out[...] = step(0)
        for j in range(SAVES):
            save(j).wait()


def chain(prompt, active, g, stash, probs, k, v):
    n, rows, _ = probs.shape
    anywhere = pl.BlockSpec(memory_space=pl.ANY)
    return pl.pallas_call(
        functools.partial(chain_kernel, prompt),
        name="prompt_chain" if prompt else "response_chain",
        cost_estimate=about(7),
        in_specs=[SMEM, VMEM, anywhere] + [HBM] * 3,
        out_specs=[VMEM, anywhere],
        scratch_shapes=[
            pltpu.VMEM(probs.shape, f32),
            pltpu.VMEM(k.shape, bf16),
            pltpu.VMEM(v.shape, bf16),
            pltpu.VMEM((n, rows, HD), bf16),
            pltpu.SemaphoreType.DMA((len(GROUPS), 3)),
            pltpu.SemaphoreType.DMA((SAVES,)),
        ],
        out_shape=[shape((rows, HD), bf16), shape((n, rows, HD), bf16)],
        input_output_aliases={2: 1},
        compiler_params=params(22),
    )(active, g, stash, in_hbm(probs), in_hbm(k), in_hbm(v))


HEADS_AT_ONCE = 2


def own_prob_kernel(prompt, active, lens, q_ref, k_ref, *refs):
    out, probs, queries, bias, sems, q_sem = refs[-6:]
    steps = queries.shape[0] // AT_ONCE

    def done(i):
        some = pl.ds(i * AT_ONCE, AT_ONCE) if prompt else pl.ds(i, 1)
        return pltpu.make_async_copy(probs.at[some], out.at[some], sems.at[i])

    @pl.when(active[0] == 1)
    def _():
        fetch = pltpu.make_async_copy(q_ref, queries, q_sem)
        fetch.start()
        if prompt:
            bias[...] = prompt_bias(1)
        else:
            bias[...] = response_bias(lens, 1, AT_ONCE)
        k1, k2 = k_ref[:PROMPT], k_ref[PROMPT:]
        fetch.wait()

        def body(i, carry):
            if prompt:
                for u in range(AT_ONCE):
                    head = i * AT_ONCE + u
                    (probs[head],) = softmax([dot_nt(k1, queries[head]) + bias[...]], 0)
            else:
                q = queries[pl.ds(i * AT_ONCE, AT_ONCE)].reshape(AT_ONCE * RESP, HD)
                p1, p2 = softmax([dot_nt(k1, q), dot_nt(k2, q) + bias[...]], 0)
                probs[i, :PROMPT] = p1
                probs[i, PROMPT:] = p2
            done(i).start()
            return carry

        lax.fori_loop(0, steps, body, 0)
        for i in range(steps):
            done(i).wait()


def own_prob(prompt, active, lens, q, k, earlier=None, us=5):
    n, rows, _ = q.shape
    dims = (n, PROMPT, rows) if prompt else (n // AT_ONCE, LIVE, AT_ONCE * RESP)
    more = [] if earlier is None else [in_hbm(earlier)]
    return pl.pallas_call(
        functools.partial(own_prob_kernel, prompt),
        name="own_prompt_prob" if prompt else "own_response_prob",
        cost_estimate=about(us),
        in_specs=[SMEM, SMEM, HBM, VMEM] + [HBM] * len(more),
        out_specs=HBM,
        scratch_shapes=[
            pltpu.VMEM(dims, f32),
            pltpu.VMEM(q.shape, bf16),
            pltpu.VMEM((rows, rows if prompt else AT_ONCE * RESP), f32),
            pltpu.SemaphoreType.DMA((n // AT_ONCE,)),
            pltpu.SemaphoreType.DMA,
        ],
        out_shape=pltpu.HBM(dims, f32),
        input_output_aliases={4: 0} if more else {},
        compiler_params=params(16),
    )(active, lens, in_hbm(q), k, *more)


def prompt_grad_kernel(probs, q_ref, g_ref, v_ref, out_ref):
    @pl.when(pl.program_id(0) == 0)
    def _():
        out_ref[...] = jnp.zeros_like(out_ref)

    v = v_ref[...]

    def body(j, carry):
        dk, dv = 0.0, 0.0
        for i in range(HEADS_AT_ONCE):
            u = j * HEADS_AT_ONCE + i
            q, g, p = q_ref[u], g_ref[u], probs[u]
            dp = dot_nt(v, g)
            pb = p.astype(bf16)
            delta = jnp.sum(pb.astype(f32) * dp, 0, keepdims=True)
            ds = (p * (dp - delta)).astype(bf16)
            dk = dk + dot(ds, q)
            dv = dv + dot(pb, g)
        out_ref[:, :HD] += dk * SCALE
        out_ref[:, HD:] += dv
        return carry

    lax.fori_loop(0, q_ref.shape[0] // HEADS_AT_ONCE, body, 0)


def prompt_grad(probs, q, g, v):
    n = q.shape[0]
    block = lambda *dims: pl.BlockSpec((AT_ONCE,) + dims, lambda i: (i, 0, 0))
    whole = lambda *dims: pl.BlockSpec(dims, lambda i: (0, 0))
    return pl.pallas_call(
        prompt_grad_kernel,
        name="prompt_grad",
        cost_estimate=about(5),
        grid=(n // AT_ONCE,),
        in_specs=[
            block(PROMPT, PROMPT),
            block(PROMPT, HD),
            block(PROMPT, HD),
            whole(PROMPT, HD),
        ],
        out_specs=whole(PROMPT, 2 * HD),
        out_shape=shape((PROMPT, 2 * HD)),
        compiler_params=params(12),
    )(in_hbm(probs), q, g, v)


def response_grad_kernel(lens, probs, q_ref, g_ref, v_ref, part_ref, out_ref, sum_ref, acc):
    i = pl.program_id(0)

    @pl.when(i == 0)
    def _():
        acc[:PROMPT] = part_ref[...]
        acc[PROMPT:] = jnp.zeros((RESP, 2 * HD), f32)

    v1, v2 = v_ref[:PROMPT], v_ref[PROMPT:]
    q = q_ref[...].reshape(AT_ONCE * RESP, HD)
    g = g_ref[...].reshape(AT_ONCE * RESP, HD)
    p1, p2 = probs[0, :PROMPT], probs[0, PROMPT:]
    dp1, dp2 = dot_nt(v1, g), dot_nt(v2, g)
    pb1, pb2 = p1.astype(bf16), p2.astype(bf16)
    delta = jnp.sum(pb1.astype(f32) * dp1, 0, keepdims=True) + jnp.sum(
        pb2.astype(f32) * dp2, 0, keepdims=True
    )
    ds1 = (p1 * (dp1 - delta)).astype(bf16)
    ds2 = (p2 * (dp2 - delta)).astype(bf16)
    acc[:PROMPT, :HD] += dot(ds1, q) * SCALE
    acc[PROMPT:, :HD] += dot(ds2, q) * SCALE
    acc[:PROMPT, HD:] += dot(pb1, g)
    acc[PROMPT:, HD:] += dot(pb2, g)

    @pl.when(i == pl.num_programs(0) - 1)
    def _():
        total = acc[...]
        squares = jnp.sum(total * total, 0, keepdims=True)
        sum_ref[...] = squares[:, :HD] + squares[:, HD:]
        out_ref[:PROMPT] = total[:PROMPT]
        left = total[PROMPT:]
        spread = chosen_rows(lens, 1)
        placed = jnp.zeros((NRESP * RLEN, 2 * HD), f32)
        for _ in range(3):
            term = left.astype(bf16)
            placed = placed + dot(spread, term)
            left = left - term.astype(f32)
        out_ref[PROMPT:] = placed


def response_grad(lens, probs, q, g, v, part):
    n = q.shape[0]
    rows = PROMPT + NRESP * RLEN
    block = lambda *dims: pl.BlockSpec((AT_ONCE,) + dims, lambda i, a: (i, 0, 0))
    whole = lambda *dims: pl.BlockSpec(dims, lambda i, a: (0, 0))
    return pl.pallas_call(
        response_grad_kernel,
        name="response_grad",
        cost_estimate=about(8),
        grid_spec=pltpu.PrefetchScalarGridSpec(
            num_scalar_prefetch=1,
            grid=(n // AT_ONCE,),
            in_specs=[
                pl.BlockSpec((1, LIVE, AT_ONCE * RESP), lambda i, a: (i, 0, 0)),
                block(RESP, HD),
                block(RESP, HD),
                whole(LIVE, HD),
                whole(PROMPT, 2 * HD),
            ],
            out_specs=[whole(rows, 2 * HD), whole(1, HD)],
            scratch_shapes=[pltpu.VMEM((LIVE, 2 * HD), f32)],
        ),
        out_shape=[shape((rows, 2 * HD)), shape((1, HD))],
        compiler_params=params(12),
    )(lens, in_hbm(probs), q, g, v, part)


def ring(step, size=SIDE):
    return [(i, (i + step) % size) for i in range(size)]


def gathered(block, axis):
    return [block] + [lax.ppermute(block, axis, ring(step)) for step in (1, -1, 2)]


def gathered_halves(block, axis):
    low, high = (lax.ppermute(block, axis, ring(step)) for step in (1, -1))
    half = block.shape[0] // 2
    return [
        block,
        low,
        high,
        lax.ppermute(low[:half], axis, ring(1)),
        lax.ppermute(high[half:], axis, ring(-1)),
    ]


def on_device(hidden_stash, key_stash, value_stash, top_grads, lens):
    stage = lax.axis_index("zl")
    my_x = lax.axis_index("x")
    my_y = lax.axis_index("y")
    place = (my_x * SIDE + my_y).reshape(1).astype(jnp.int32)
    qp, qr, gp, gr = pack(lens, place, hidden_stash[0], top_grads)
    parts = jnp.arange(PLANE, dtype=jnp.int32)
    away = lambda slot: jnp.where(slot == 1, 3, jnp.where(slot == 2, 1, jnp.where(slot == 3, 2, 0)))
    outer, inner = away(parts // SIDE), away(parts % SIDE)
    k_from = ((my_x + outer) % SIDE * SIDE + (my_y + inner) % SIDE).astype(jnp.int32)
    v_from = ((my_x + inner) % SIDE * SIDE + (my_y + outer) % SIDE).astype(jnp.int32)
    plane = ("x", "y")
    swap = lambda a: lax.all_to_all(a, plane, 0, 0, tiled=True)
    after = lambda x, y: lax.optimization_barrier((x, y))[0]
    row_k, col_v = stack_live(
        lens, gathered(key_stash[0], "y"), gathered(value_stash[0], "x")
    )
    row_k, col_v, qp = lax.optimization_barrier((row_k, col_v, qp))
    k, v = row_k[0], col_v[0]
    my_qp = swap(qp)
    all_k = gathered_halves(row_k, "x")
    all_v = gathered_halves(col_v, "y")
    my_qr = swap(after(qr, my_qp))
    prob_p, key_p, value_p = prob(True, lens, k_from, v_from, my_qp, all_k, all_v)
    prob_r, key_r, value_r = prob(False, lens, k_from, v_from, my_qr, all_k, all_v)
    stash_p, stash_r = my_qp, my_qr
    busy = (stage >= STAGES // 2).astype(jnp.int32).reshape(1)
    actives = [(stage == now).astype(jnp.int32).reshape(1) for now in range(STAGES)]
    lower = lambda a: lax.ppermute(a, "zl", [(now, now - 1)])
    for now in range(STAGES - 1, -1, -1):
        if now:
            gp, stash_p = chain(True, actives[now], gp, stash_p, prob_p, key_p, value_p)
            if now == STAGES - 2:
                own_p = own_prob(True, 1 - busy, lens, after(qp, gp), k)
                own_r = own_prob(False, 1 - busy, lens, after(qr, own_p), k)
            sent = lower(gp)
            gr = after(gr, gp if now == STAGES - 1 else sent)
            gp = sent
        if now == 1:
            gp, stash_p = chain(True, actives[0], gp, stash_p, prob_p, key_p, value_p)
            own_gp = swap(stash_p)
            gr = after(gr, stash_p)
        gr, stash_r = chain(False, actives[now], gr, stash_r, prob_r, key_r, value_r)
        if now == STAGES - 2:
            gp = after(gp, own_r)
        if now:
            gp = after(gp, gr)
            gr = lower(gr)
    own_p = own_prob(True, busy, lens, after(qp, gr), k, own_p)
    own_gr = swap(stash_r)
    part = prompt_grad(after(own_p, gr), qp, own_gp, v)
    own_r = own_prob(False, busy, lens, after(qr, part), k, own_r)
    raw, squares = response_grad(lens, own_r, qr, own_gr, v, part)
    for axes in (("x", "y", "core"), ("zl", "zh")):
        size = lax.axis_size(axes)
        spread = jnp.broadcast_to(squares, (size, HD))
        squares = jnp.sum(lax.all_to_all(spread, axes, 0, 0, tiled=True), 0, keepdims=True)
    square_sum = jnp.sum(squares)
    entries = STAGES * PLANE * lax.axis_size(("zh", "core")) * raw.shape[0] * raw.shape[1]
    clip_limit = clip_rms * math.sqrt(entries)
    factor = clip_limit / jnp.maximum(jnp.sqrt(square_sum), clip_limit)
    return (raw * factor)[None]


def solution(mesh):
    parts = mesh.devices.reshape(STAGES, SIDE, SIDE, 2, -1)
    finer = Mesh(parts, ("zl", "x", "y", "zh", "core"))
    tp = ("zh", "core")
    pipe = ("zl", "x", "y")
    placed = (
        P(pipe, None, tp),
        P(pipe, None, tp),
        P(pipe, None, tp),
        P(None, tp),
        P(),
    )
    return jax.shard_map(
        on_device, mesh=finer, in_specs=placed, out_specs=P(pipe, None, tp), check_vma=False
    )
```

```python
import functools
import math

import jax
import jax.numpy as jnp
from jax import lax
from jax.experimental import pallas as pl
from jax.experimental.pallas import tpu as pltpu
from jax.sharding import Mesh, PartitionSpec as P

HD = 128
PROMPT = 256
NRESP = 4
RLEN = 64
RESP = 192
LIVE = PROMPT + RESP
STAGES = 4
SIDE = 4
PLANE = SIDE * SIDE

clip_rms = 0.5
SCALE = 1.0 / math.sqrt(HD)
EXP2_SCALE = SCALE * math.log2(math.e)
f32 = jnp.float32
bf16 = jnp.bfloat16


VMEM = pl.BlockSpec(memory_space=pltpu.VMEM)
SMEM = pl.BlockSpec(memory_space=pltpu.SMEM)
HBM = pl.BlockSpec(memory_space=pltpu.HBM)


def dot(a, b):
    return lax.dot_general(a, b, (((1,), (0,)), ((), ())), preferred_element_type=f32)


def dot_nt(a, b):
    return lax.dot_general(a, b, (((1,), (1,)), ((), ())), preferred_element_type=f32)


def about(us):
    return pl.CostEstimate(flops=us * 1_000_000_000, bytes_accessed=0, transcendentals=0)


def params(mebibytes=24):
    return pltpu.CompilerParams(vmem_limit_bytes=mebibytes << 20)


def shape(dims, dtype=f32):
    return jax.ShapeDtypeStruct(dims, dtype)


def starts(lens):
    first = lens[0]
    second = first + lens[1]
    return first, second, second + lens[2]


def start_of(row, lens):
    one, two, three = starts(lens)
    return jnp.where(
        row >= three, three, jnp.where(row >= two, two, jnp.where(row >= one, one, 0))
    )


def prompt_bias(query_dim):
    q = lax.broadcasted_iota(jnp.int32, (PROMPT, PROMPT), query_dim)
    k = lax.broadcasted_iota(jnp.int32, (PROMPT, PROMPT), 1 - query_dim)
    return jnp.where(k <= q, 0.0, -jnp.inf).astype(f32)


def response_bias(lens, query_dim, repeats=1):
    dims = (RESP, repeats * RESP)
    q = lax.broadcasted_iota(jnp.int32, dims, query_dim)
    k = lax.broadcasted_iota(jnp.int32, dims, 1 - query_dim)
    for _ in range(repeats - 1):
        q = jnp.where(q >= RESP, q - RESP, q)
    return jnp.where((k <= q) & (k >= start_of(q, lens)), 0.0, -jnp.inf).astype(f32)


def chosen_rows(lens, row_dim):
    dims = (RESP, NRESP * RLEN) if row_dim == 0 else (NRESP * RLEN, RESP)
    row = lax.broadcasted_iota(jnp.int32, dims, row_dim)
    col = lax.broadcasted_iota(jnp.int32, dims, 1 - row_dim)
    one, two, three = starts(lens)
    slot = (
        (row >= one).astype(jnp.int32)
        + (row >= two).astype(jnp.int32)
        + (row >= three).astype(jnp.int32)
    )
    return jnp.where(col == slot * RLEN + row - start_of(row, lens), 1.0, 0.0).astype(bf16)


def pack_kernel(lens, place, x_ref, top_ref, xp_out, xr_out, tp_out, tr_out, chosen):
    @pl.when(pl.program_id(0) == 0)
    def _():
        pick = chosen_rows(lens, 0)
        chosen[...] = pick
        tp_out[...] = top_ref[:PROMPT]
        tr_out[...] = dot(pick, top_ref[PROMPT:]).astype(bf16)

    live = dot(chosen[...], x_ref[PROMPT:]).astype(bf16)
    for h in range(x_ref.shape[1] // HD):
        cols = slice(h * HD, (h + 1) * HD)
        xp_out[h] = x_ref[:PROMPT, cols]
        xr_out[h] = live[:, cols]


def pack(lens, place, x, top):
    rows, width = x.shape
    heads = width // HD
    steps = 2
    some = heads // steps
    whole = lambda n: pl.BlockSpec((n, HD), lambda i, l, p: (0, 0))
    return pl.pallas_call(
        pack_kernel,
        name="pack",
        cost_estimate=about(4),
        grid_spec=pltpu.PrefetchScalarGridSpec(
            num_scalar_prefetch=2,
            grid=(steps,),
            in_specs=[
                pl.BlockSpec((rows, some * HD), lambda i, l, p: (0, i)),
                pl.BlockSpec((rows, HD), lambda i, l, p: (0, p[0])),
            ],
            out_specs=[
                pl.BlockSpec((some, PROMPT, HD), lambda i, l, p: (i, 0, 0)),
                pl.BlockSpec((some, RESP, HD), lambda i, l, p: (i, 0, 0)),
                whole(PROMPT),
                whole(RESP),
            ],
            scratch_shapes=[pltpu.VMEM((RESP, NRESP * RLEN), bf16)],
        ),
        out_shape=[
            shape((heads, PROMPT, HD), bf16),
            shape((heads, RESP, HD), bf16),
            shape((PROMPT, HD), bf16),
            shape((RESP, HD), bf16),
        ],
        compiler_params=params(60),
    )(lens, place, x, top)


def stack_live_kernel(lens, *refs):
    out_k, out_v = refs[2 * SIDE :]
    chosen = chosen_rows(lens, 0)
    for parts, out in ((refs[:SIDE], out_k), (refs[SIDE : 2 * SIDE], out_v)):
        for i, part in enumerate(parts):
            out[i, :PROMPT] = part[:PROMPT]
            out[i, PROMPT:] = dot(chosen, part[PROMPT:]).astype(bf16)


def stack_live(lens, keys, values):
    return pl.pallas_call(
        stack_live_kernel,
        name="stack_live",
        cost_estimate=about(2),
        in_specs=[SMEM] + [VMEM] * (2 * SIDE),
        out_specs=[VMEM] * 2,
        out_shape=[shape((SIDE, LIVE, HD), bf16)] * 2,
        compiler_params=params(8),
    )(lens, *keys, *values)


def softmax(scores, dim):
    top = functools.reduce(jnp.maximum, [jnp.max(x, dim, keepdims=True) for x in scores])
    weights = [jnp.exp2((x - top) * EXP2_SCALE) for x in scores]
    total = functools.reduce(jnp.add, [jnp.sum(w, dim, keepdims=True) for w in weights])
    share = 1.0 / total
    return [w * share for w in weights]


AT_ONCE = 4
SENT = 1
PROMPT_ROW = PROMPT + HD
RESP_ROW = 2 * PROMPT + HD
def in_hbm(x):
    return pltpu.with_memory_space_constraint(x, pltpu.HBM)


def prob_kernel(prompt, lens, k_from, v_from, q_ref, *refs):
    half = (len(refs) - 9) // 2
    k_parts, v_parts = refs[:half], refs[half : 2 * half]
    probs_out, keys_out, values_out, probs, keys, values, bias, sems, kv_sems = refs[2 * half :]
    n, count, _ = keys.shape
    bias[...] = prompt_bias(0) if prompt else response_bias(lens, 0)
    for parts, held, table in ((k_parts, keys, k_from), (v_parts, values, v_from)):
        at = 0
        for part in parts:
            for i in range(part.shape[0]):
                held[table[at]] = part[i, :count]
                at += 1
    ordered = [
        pltpu.make_async_copy(held, out, kv_sems.at[j])
        for j, (held, out) in enumerate(((keys, keys_out), (values, values_out)))
    ]
    for copy in ordered:
        copy.start()

    def done(i):
        some = pl.ds(i * SENT, SENT)
        return pltpu.make_async_copy(probs.at[some], probs_out.at[some], sems.at[i])

    def body(i, carry):
        for u in range(AT_ONCE):
            layer = i * AT_ONCE + u
            q, k, v = q_ref[layer], keys[layer], values[layer]
            if prompt:
                (p,) = softmax([dot_nt(q, k) + bias[...]], -1)
                probs[layer, :, :PROMPT] = p
                probs[layer, :, PROMPT:] = dot(p.astype(bf16), v)
            else:
                p1, p2 = softmax([dot_nt(q, k[:PROMPT]), dot_nt(q, k[PROMPT:]) + bias[...]], -1)
                probs[layer, :, :PROMPT] = p1
                probs[layer, :, PROMPT:LIVE] = p2
                probs[layer, :, 2 * PROMPT :] = dot(p1.astype(bf16), v[:PROMPT]) + dot(
                    p2.astype(bf16), v[PROMPT:]
                )
            if u % SENT == SENT - 1:
                done(i * (AT_ONCE // SENT) + u // SENT).start()
        return carry

    lax.fori_loop(0, n // AT_ONCE, body, 0)
    for copy in ordered + [done(i) for i in range(n // SENT)]:
        copy.wait()


def prob(prompt, lens, k_from, v_from, q, k, v):
    n, rows, _ = q.shape
    count, width = (PROMPT, PROMPT_ROW) if prompt else (LIVE, RESP_ROW)
    results = [((n, rows, width), f32), ((n, count, HD), bf16), ((n, count, HD), bf16)]
    return pl.pallas_call(
        functools.partial(prob_kernel, prompt),
        name="prompt_prob" if prompt else "response_prob",
        cost_estimate=about(7),
        in_specs=[SMEM] * 3 + [VMEM] * (1 + len(k) + len(v)),
        out_specs=[HBM] * 3,
        scratch_shapes=[pltpu.VMEM(*r) for r in results]
        + [
            pltpu.VMEM((rows, rows), f32),
            pltpu.SemaphoreType.DMA((n // SENT,)),
            pltpu.SemaphoreType.DMA((2,)),
        ],
        out_shape=[pltpu.HBM(*r) for r in results],
        compiler_params=params(22),
    )(lens, k_from, v_from, q, *k, *v)


GROUPS = ((15, 16), (14, 15), (12, 14), (10, 12), (8, 10), (6, 8), (4, 6), (2, 4), (0, 2))
AHEAD = 4
SAVES = 4


def chain_kernel(prompt, active, g_in, stash_in, probs_in, keys_in, values_in, g_out, stash, probs, keys, values, grads, sems, save_sems):
    n = keys.shape[0]

    def loads(j):
        span = pl.ds(GROUPS[j][0], GROUPS[j][1] - GROUPS[j][0])
        return [
            pltpu.make_async_copy(source.at[span], held.at[span], sems.at[j, i])
            for i, (source, held) in enumerate(
                ((values_in, values), (probs_in, probs), (keys_in, keys))
            )
        ]

    def step(layer):
        d = grads[layer]
        wide = d.astype(f32)
        k, v = keys[layer], values[layer]
        if prompt:
            delta = jnp.sum(wide * probs[layer, :, PROMPT:], -1, keepdims=True)
            ds = (probs[layer, :, :PROMPT] * (dot_nt(d, v) - delta)).astype(bf16)
            change = dot(ds, k)
        else:
            delta = jnp.sum(wide * probs[layer, :, 2 * PROMPT :], -1, keepdims=True)
            ds1 = (probs[layer, :, :PROMPT] * (dot_nt(d, v[:PROMPT]) - delta)).astype(bf16)
            ds2 = (probs[layer, :, PROMPT:LIVE] * (dot_nt(d, v[PROMPT:]) - delta)).astype(bf16)
            change = dot(ds1, k[:PROMPT]) + dot(ds2, k[PROMPT:])
        return (wide + change * SCALE).astype(bf16)

    def save(j):
        some = pl.ds(j * (n // SAVES), n // SAVES)
        return pltpu.make_async_copy(grads.at[some], stash.at[some], save_sems.at[j])

    @pl.when(active[0] == 1)
    def _():
        for j in range(AHEAD):
            for copy in loads(j):
                copy.start()
        grads[n - 1] = g_in[...]
        for j, (low, high) in enumerate(GROUPS):
            for copy in loads(j):
                copy.wait()
            if j + AHEAD < len(GROUPS):
                for copy in loads(j + AHEAD):
                    copy.start()

            def body(i, carry, high=high):
                grads[high - 2 - i] = step(high - 1 - i)
                return carry

            if high - low == 1:
                body(0, 0)
            else:
                lax.fori_loop(0, high - max(low, 1), body, 0)
            if low and low % (n // SAVES) == 0:
                save(low // (n // SAVES)).start()
        save(0).start()
        g_out[...] = step(0)
        for j in range(SAVES):
            save(j).wait()


def chain(prompt, active, g, stash, probs, k, v):
    n, rows, _ = probs.shape
    anywhere = pl.BlockSpec(memory_space=pl.ANY)
    return pl.pallas_call(
        functools.partial(chain_kernel, prompt),
        name="prompt_chain" if prompt else "response_chain",
        cost_estimate=about(7),
        in_specs=[SMEM, VMEM, anywhere] + [HBM] * 3,
        out_specs=[VMEM, anywhere],
        scratch_shapes=[
            pltpu.VMEM(probs.shape, f32),
            pltpu.VMEM(k.shape, bf16),
            pltpu.VMEM(v.shape, bf16),
            pltpu.VMEM((n, rows, HD), bf16),
            pltpu.SemaphoreType.DMA((len(GROUPS), 3)),
            pltpu.SemaphoreType.DMA((SAVES,)),
        ],
        out_shape=[shape((rows, HD), bf16), shape((n, rows, HD), bf16)],
        input_output_aliases={2: 1},
        compiler_params=params(22),
    )(active, g, stash, in_hbm(probs), in_hbm(k), in_hbm(v))


HEADS_AT_ONCE = 2


def own_prob_kernel(prompt, active, lens, q_ref, k_ref, *refs):
    out, probs, queries, bias, sems, q_sem = refs[-6:]
    steps = queries.shape[0] // AT_ONCE

    def done(i):
        some = pl.ds(i * AT_ONCE, AT_ONCE) if prompt else pl.ds(i, 1)
        return pltpu.make_async_copy(probs.at[some], out.at[some], sems.at[i])

    @pl.when(active[0] == 1)
    def _():
        fetch = pltpu.make_async_copy(q_ref, queries, q_sem)
        fetch.start()
        if prompt:
            bias[...] = prompt_bias(1)
        else:
            bias[...] = response_bias(lens, 1, AT_ONCE)
        k1, k2 = k_ref[:PROMPT], k_ref[PROMPT:]
        fetch.wait()

        def body(i, carry):
            if prompt:
                for u in range(AT_ONCE):
                    head = i * AT_ONCE + u
                    (probs[head],) = softmax([dot_nt(k1, queries[head]) + bias[...]], 0)
            else:
                q = queries[pl.ds(i * AT_ONCE, AT_ONCE)].reshape(AT_ONCE * RESP, HD)
                p1, p2 = softmax([dot_nt(k1, q), dot_nt(k2, q) + bias[...]], 0)
                probs[i, :PROMPT] = p1
                probs[i, PROMPT:] = p2
            done(i).start()
            return carry

        lax.fori_loop(0, steps, body, 0)
        for i in range(steps):
            done(i).wait()


def own_prob(prompt, active, lens, q, k, earlier=None, us=5):
    n, rows, _ = q.shape
    dims = (n, PROMPT, rows) if prompt else (n // AT_ONCE, LIVE, AT_ONCE * RESP)
    more = [] if earlier is None else [in_hbm(earlier)]
    return pl.pallas_call(
        functools.partial(own_prob_kernel, prompt),
        name="own_prompt_prob" if prompt else "own_response_prob",
        cost_estimate=about(us),
        in_specs=[SMEM, SMEM, HBM, VMEM] + [HBM] * len(more),
        out_specs=HBM,
        scratch_shapes=[
            pltpu.VMEM(dims, f32),
            pltpu.VMEM(q.shape, bf16),
            pltpu.VMEM((rows, rows if prompt else AT_ONCE * RESP), f32),
            pltpu.SemaphoreType.DMA((n // AT_ONCE,)),
            pltpu.SemaphoreType.DMA,
        ],
        out_shape=pltpu.HBM(dims, f32),
        input_output_aliases={4: 0} if more else {},
        compiler_params=params(16),
    )(active, lens, in_hbm(q), k, *more)


def prompt_grad_kernel(probs, q_ref, g_ref, v_ref, out_ref):
    @pl.when(pl.program_id(0) == 0)
    def _():
        out_ref[...] = jnp.zeros_like(out_ref)

    v = v_ref[...]

    def body(j, carry):
        dk, dv = 0.0, 0.0
        for i in range(HEADS_AT_ONCE):
            u = j * HEADS_AT_ONCE + i
            q, g, p = q_ref[u], g_ref[u], probs[u]
            dp = dot_nt(v, g)
            pb = p.astype(bf16)
            delta = jnp.sum(pb.astype(f32) * dp, 0, keepdims=True)
            ds = (p * (dp - delta)).astype(bf16)
            dk = dk + dot(ds, q)
            dv = dv + dot(pb, g)
        out_ref[:, :HD] += dk * SCALE
        out_ref[:, HD:] += dv
        return carry

    lax.fori_loop(0, q_ref.shape[0] // HEADS_AT_ONCE, body, 0)


def prompt_grad(probs, q, g, v):
    n = q.shape[0]
    block = lambda *dims: pl.BlockSpec((AT_ONCE,) + dims, lambda i: (i, 0, 0))
    whole = lambda *dims: pl.BlockSpec(dims, lambda i: (0, 0))
    return pl.pallas_call(
        prompt_grad_kernel,
        name="prompt_grad",
        cost_estimate=about(5),
        grid=(n // AT_ONCE,),
        in_specs=[
            block(PROMPT, PROMPT),
            block(PROMPT, HD),
            block(PROMPT, HD),
            whole(PROMPT, HD),
        ],
        out_specs=whole(PROMPT, 2 * HD),
        out_shape=shape((PROMPT, 2 * HD)),
        compiler_params=params(12),
    )(in_hbm(probs), q, g, v)


def response_grad_kernel(lens, probs, q_ref, g_ref, v_ref, part_ref, out_ref, sum_ref, acc):
    i = pl.program_id(0)

    @pl.when(i == 0)
    def _():
        acc[:PROMPT] = part_ref[...]
        acc[PROMPT:] = jnp.zeros((RESP, 2 * HD), f32)

    v1, v2 = v_ref[:PROMPT], v_ref[PROMPT:]
    q = q_ref[...].reshape(AT_ONCE * RESP, HD)
    g = g_ref[...].reshape(AT_ONCE * RESP, HD)
    p1, p2 = probs[0, :PROMPT], probs[0, PROMPT:]
    dp1, dp2 = dot_nt(v1, g), dot_nt(v2, g)
    pb1, pb2 = p1.astype(bf16), p2.astype(bf16)
    delta = jnp.sum(pb1.astype(f32) * dp1, 0, keepdims=True) + jnp.sum(
        pb2.astype(f32) * dp2, 0, keepdims=True
    )
    ds1 = (p1 * (dp1 - delta)).astype(bf16)
    ds2 = (p2 * (dp2 - delta)).astype(bf16)
    acc[:PROMPT, :HD] += dot(ds1, q) * SCALE
    acc[PROMPT:, :HD] += dot(ds2, q) * SCALE
    acc[:PROMPT, HD:] += dot(pb1, g)
    acc[PROMPT:, HD:] += dot(pb2, g)

    @pl.when(i == pl.num_programs(0) - 1)
    def _():
        total = acc[...]
        squares = jnp.sum(total * total, 0, keepdims=True)
        sum_ref[...] = squares[:, :HD] + squares[:, HD:]
        out_ref[:PROMPT] = total[:PROMPT]
        left = total[PROMPT:]
        spread = chosen_rows(lens, 1)
        placed = jnp.zeros((NRESP * RLEN, 2 * HD), f32)
        for _ in range(3):
            term = left.astype(bf16)
            placed = placed + dot(spread, term)
            left = left - term.astype(f32)
        out_ref[PROMPT:] = placed


def response_grad(lens, probs, q, g, v, part):
    n = q.shape[0]
    rows = PROMPT + NRESP * RLEN
    block = lambda *dims: pl.BlockSpec((AT_ONCE,) + dims, lambda i, a: (i, 0, 0))
    whole = lambda *dims: pl.BlockSpec(dims, lambda i, a: (0, 0))
    return pl.pallas_call(
        response_grad_kernel,
        name="response_grad",
        cost_estimate=about(8),
        grid_spec=pltpu.PrefetchScalarGridSpec(
            num_scalar_prefetch=1,
            grid=(n // AT_ONCE,),
            in_specs=[
                pl.BlockSpec((1, LIVE, AT_ONCE * RESP), lambda i, a: (i, 0, 0)),
                block(RESP, HD),
                block(RESP, HD),
                whole(LIVE, HD),
                whole(PROMPT, 2 * HD),
            ],
            out_specs=[whole(rows, 2 * HD), whole(1, HD)],
            scratch_shapes=[pltpu.VMEM((LIVE, 2 * HD), f32)],
        ),
        out_shape=[shape((rows, 2 * HD)), shape((1, HD))],
        compiler_params=params(12),
    )(lens, in_hbm(probs), q, g, v, part)


def ring(step, size=SIDE):
    return [(i, (i + step) % size) for i in range(size)]


def gathered(block, axis):
    return [block] + [lax.ppermute(block, axis, ring(step)) for step in (1, -1, 2)]


def gathered_halves(block, axis):
    low, high = (lax.ppermute(block, axis, ring(step)) for step in (1, -1))
    half = block.shape[0] // 2
    return [
        block,
        low,
        high,
        lax.ppermute(low[:half], axis, ring(1)),
        lax.ppermute(high[half:], axis, ring(-1)),
    ]


def on_device(hidden_stash, key_stash, value_stash, top_grads, lens):
    stage = lax.axis_index("zl")
    my_x = lax.axis_index("x")
    my_y = lax.axis_index("y")
    place = (my_x * SIDE + my_y).reshape(1).astype(jnp.int32)
    qp, qr, gp, gr = pack(lens, place, hidden_stash[0], top_grads)
    parts = jnp.arange(PLANE, dtype=jnp.int32)
    away = lambda slot: jnp.where(slot == 1, 3, jnp.where(slot == 2, 1, jnp.where(slot == 3, 2, 0)))
    outer, inner = away(parts // SIDE), away(parts % SIDE)
    k_from = ((my_x + outer) % SIDE * SIDE + (my_y + inner) % SIDE).astype(jnp.int32)
    v_from = ((my_x + inner) % SIDE * SIDE + (my_y + outer) % SIDE).astype(jnp.int32)
    plane = ("x", "y")
    swap = lambda a: lax.all_to_all(a, plane, 0, 0, tiled=True)
    after = lambda x, y: lax.optimization_barrier((x, y))[0]
    row_k, col_v = stack_live(
        lens, gathered(key_stash[0], "y"), gathered(value_stash[0], "x")
    )
    row_k, col_v, qp = lax.optimization_barrier((row_k, col_v, qp))
    k, v = row_k[0], col_v[0]
    my_qp = swap(qp)
    all_k = gathered_halves(row_k, "x")
    all_v = gathered_halves(col_v, "y")
    my_qr = swap(after(qr, my_qp))
    prob_p, key_p, value_p = prob(True, lens, k_from, v_from, my_qp, all_k, all_v)
    prob_r, key_r, value_r = prob(False, lens, k_from, v_from, my_qr, all_k, all_v)
    stash_p, stash_r = my_qp, my_qr
    busy = (stage >= STAGES // 2).astype(jnp.int32).reshape(1)
    actives = [(stage == now).astype(jnp.int32).reshape(1) for now in range(STAGES)]
    lower = lambda a: lax.ppermute(a, "zl", [(now, now - 1)])
    for now in range(STAGES - 1, -1, -1):
        if now:
            gp, stash_p = chain(True, actives[now], gp, stash_p, prob_p, key_p, value_p)
            if now == STAGES - 2:
                own_p = own_prob(True, 1 - busy, lens, after(qp, gp), k)
                own_r = own_prob(False, 1 - busy, lens, after(qr, own_p), k)
            sent = lower(gp)
            gr = after(gr, gp if now == STAGES - 1 else sent)
            gp = sent
        if now == 1:
            gp, stash_p = chain(True, actives[0], gp, stash_p, prob_p, key_p, value_p)
            own_gp = swap(stash_p)
            gr = after(gr, stash_p)
        gr, stash_r = chain(False, actives[now], gr, stash_r, prob_r, key_r, value_r)
        if now == STAGES - 2:
            gp = after(gp, own_r)
        if now:
            gp = after(gp, gr)
            gr = lower(gr)
    own_p = own_prob(True, busy, lens, after(qp, gr), k, own_p)
    own_gr = swap(stash_r)
    part = prompt_grad(after(own_p, gr), qp, own_gp, v)
    own_r = own_prob(False, busy, lens, after(qr, part), k, own_r)
    raw, squares = response_grad(lens, own_r, qr, own_gr, v, part)
    for axes in (("x", "y", "core"), ("zl", "zh")):
        size = lax.axis_size(axes)
        spread = jnp.broadcast_to(squares, (size, HD))
        squares = jnp.sum(lax.all_to_all(spread, axes, 0, 0, tiled=True), 0, keepdims=True)
    square_sum = jnp.sum(squares)
    entries = STAGES * PLANE * lax.axis_size(("zh", "core")) * raw.shape[0] * raw.shape[1]
    clip_limit = clip_rms * math.sqrt(entries)
    factor = clip_limit / jnp.maximum(jnp.sqrt(square_sum), clip_limit)
    return (raw * factor)[None]


def solution(mesh):
    parts = mesh.devices.reshape(STAGES, SIDE, SIDE, 2, -1)
    finer = Mesh(parts, ("zl", "x", "y", "zh", "core"))
    tp = ("zh", "core")
    pipe = ("zl", "x", "y")
    placed = (
        P(pipe, None, tp),
        P(pipe, None, tp),
        P(pipe, None, tp),
        P(None, tp),
        P(),
    )
    return jax.shard_map(
        on_device, mesh=finer, in_specs=placed, out_specs=P(pipe, None, tp), check_vma=False
    )
```
